512 devices in a mesh: seq: 64 (over z, y), ch: 8 (over x, core).
Axes of the slice: x: 4, y: 8, z: 8, core: 2. Of those that a mesh axis runs over, the one named last changes fastest.
Arguments:
- upstream_grad: bfloat16 [8192, 4096], P('seq', 'ch'), may hold values from -6 to 6
- gate_act: bfloat16 [8192, 4096], P('seq', 'ch'), may hold values from -6 to 6
- value_act: bfloat16 [8192, 4096], P('seq', 'ch'), may hold values from -0.5 to 0.5
- filter_taps: bfloat16 [4, 8192], P(None, 'seq'), may hold values from -6 to 6
- half_ids: int32 [128], replicated, may hold values from 0 to 127, as said below
Outputs:
- value_grad: bfloat16 [8192, 4096], P('seq', 'ch')
- filter_grad: float32 [4, 8192], P(None, 'seq')
The draws below stay inside these ranges and needn't reach their ends.
Inputs may be any that keep to these rules, and one draw needn't show every extreme that they name: `half_ids`: each value appears once; entries 2p and 2p + 1 add up to 127.
All inputs are finite; a program needn't handle non-finite values.
Results may differ from the reference program's by a relative error of at most 0.0049.
Values may be sent and summed in bfloat16 or wider, within the bound.
A program may use at most 128 MiB of HBM per device.

```python
import jax
import jax.numpy as jnp
from jax import lax

HB = 64
D = 4096
FILT = 4
L = 8192
N_SEQ = 64


def draw_half_ids(key, part):
    key = jax.random.fold_in(key, 11)
    pair_count = L // HB // 2
    lower_ids = jax.random.permutation(key, pair_count).astype(jnp.int32)
    mirror = 2 * pair_count - 1 - lower_ids
    return jnp.stack([lower_ids, mirror], axis=1).reshape(-1)


def steps_of(stream_key, extent, split, low, largest):
    loudness = 1.0
    for position, shards_of in split:
        steps = jax.random.uniform(jax.random.fold_in(jax.random.fold_in(stream_key, 6), position), (shards_of,), jnp.float32, low / len(split), largest / len(split))
        loudness = loudness * jnp.repeat(jnp.exp(steps), extent[position] // shards_of).reshape((-1,) + (1,) * (len(extent) - 1 - position))
    return loudness


def centred(own_key, extent, deviation, limit, pieces=(), held_as=jnp.bfloat16):
    result = deviation * jax.random.normal(own_key, extent, jnp.float32)
    if pieces:
        result = result * steps_of(own_key, extent, pieces, -0.22, 0.18)
    return jnp.clip(result, -limit, limit).astype(held_as)


def setup_inputs(seed: int = 0) -> dict:
    arg_keys = jax.random.split(jax.random.key(seed), 6)
    upstream_grad = centred(arg_keys[0], (L, D), 1.0, 6.0, ((0, 64), (1, 8)))
    gate_act = centred(arg_keys[1], (L, D), 1.0, 6.0, ((0, 64), (1, 8)))
    value_act = centred(arg_keys[2], (L, D), ((FILT / D) ** 0.5), 0.5, ((0, 64), (1, 8)))
    filter_taps = centred(arg_keys[3], (FILT, L), 1.0, 6.0, ((1, 64),))
    half_ids = draw_half_ids(jax.random.fold_in(arg_keys[5], 71), 0)
    return dict(upstream_grad=upstream_grad, gate_act=gate_act, value_act=value_act, filter_taps=filter_taps, half_ids=half_ids)


def reference(upstream_grad, gate_act, value_act, filter_taps, half_ids):
    halves = 2 * N_SEQ
    inverse = jnp.zeros((halves,), jnp.int32).at[half_ids].set(jnp.arange(halves, dtype=jnp.int32))
    grad_product = (upstream_grad.astype(jnp.float32) * gate_act.astype(jnp.float32)).astype(jnp.bfloat16)

    def to_global(array):
        return array.reshape(halves, HB, D)[inverse].reshape(L, D)

    grad_global = to_global(grad_product).astype(jnp.float32)
    value_global = to_global(value_act).astype(jnp.float32)
    block_width = min(D, 512)
    block_count = D // block_width
    taps_block = jnp.tile(filter_taps.astype(jnp.float32), (block_width // FILT, 1))
    fft_length = 2 * L
    taps_freq = jnp.fft.rfft(taps_block.T, n=fft_length, axis=0)

    def one_block(block_index):
        grad_cols = lax.dynamic_slice_in_dim(grad_global, block_index * block_width, block_width, 1)
        value_cols = lax.dynamic_slice_in_dim(value_global, block_index * block_width, block_width, 1)
        grad_freq = jnp.fft.rfft(grad_cols, n=fft_length, axis=0)
        value_freq = jnp.fft.rfft(value_cols, n=fft_length, axis=0)
        input_part = jnp.fft.irfft(jnp.conj(taps_freq) * grad_freq, n=fft_length, axis=0)[:L]
        lag_corr = jnp.fft.irfft(jnp.conj(value_freq) * grad_freq, n=fft_length, axis=0)[:L]
        return input_part.astype(jnp.float32), lag_corr.reshape(L, block_width // FILT, FILT).sum(1).astype(jnp.float32)

    input_parts, lag_parts = lax.map(one_block, jnp.arange(block_count, dtype=jnp.int32))
    norm_scale = 1.0 / (L ** 0.5)
    input_global = jnp.moveaxis(input_parts, 0, 1).reshape(L, D) * norm_scale
    value_grad = input_global.reshape(halves, HB, D)[half_ids].reshape(L, D).astype(jnp.bfloat16)
    filter_grad = (lag_parts.sum(0) * norm_scale).T.astype(jnp.float32)
    return value_grad, filter_grad
```

```python
import functools
import math

import jax
import jax.numpy as jnp
from jax import lax
from jax.experimental import pallas as pl
from jax.experimental.pallas import tpu as pltpu
from jax.sharding import PartitionSpec as P

MESH = pl.DeviceIdType.MESH
LANES = 128
HALF = 64
SPAN = 8


def kernel(
    seq_count,
    ch_count,
    up_ref,
    gate_ref,
    value_ref,
    taps_ref,
    ids_ref,
    vg_ref,
    fg_ref,
    row_taps,
    all_taps,
    send1,
    recv1,
    wide1,
    grad_rows,
    value_rows,
    toeplitz,
    hankel,
    lag_mat,
    out_rows,
    wide2,
    send2,
    recv2,
    part,
    parts,
    send_sems,
    recv_sems,
):
    f32, bf16 = jnp.float32, jnp.bfloat16
    y_count = 1 << ((seq_count.bit_length() - 1) // 2)
    z_count = seq_count // y_count
    me = lax.axis_index("seq")
    my_ch = lax.axis_index("ch")
    my_z, my_y = lax.div(me, y_count), lax.rem(me, y_count)
    blocks = seq_count
    live = 2 * blocks
    panels = blocks // SPAN
    norm_scale = 1.0 / math.sqrt(blocks * LANES)

    def partner(d):
        z = lax.rem(my_z + lax.div(d, y_count), z_count)
        y = lax.rem(my_y + lax.rem(d, y_count), y_count)
        return z * y_count + y

    barrier = pltpu.get_barrier_semaphore()

    def greet(d, carry):
        pl.semaphore_signal(barrier, inc=1, device_id={"seq": partner(d)}, device_id_type=MESH)
        return carry

    lax.fori_loop(1, seq_count, greet, 0)

    def greet_ch(d, carry):
        pl.semaphore_signal(
            barrier, inc=1, device_id={"ch": lax.rem(my_ch + d, ch_count)}, device_id_type=MESH
        )
        return carry

    lax.fori_loop(1, ch_count, greet_ch, 0)

    row_id = lax.broadcasted_iota(jnp.int32, (LANES, LANES), 0)
    lane_id = lax.broadcasted_iota(jnp.int32, (LANES, LANES), 1)
    flip = (row_id + lane_id == LANES - 1).astype(bf16)
    row_taps[my_y] = jnp.dot(taps_ref[...], flip, preferred_element_type=f32)

    for c in range(up_ref.shape[1] // LANES):
        cols = pl.ds(c * LANES, LANES)
        product = up_ref[:, cols].astype(f32) * gate_ref[:, cols].astype(f32)
        value = value_ref[:, cols].astype(f32)
        group = LANES // 8
        send1[pl.ds(c * group, group)] = jnp.concatenate(
            [
                product.T.reshape(group, 8, LANES),
                value.T.reshape(group, 8, LANES),
            ],
            axis=1,
        ).astype(bf16)

    pl.semaphore_wait(barrier, seq_count - 1 + ch_count - 1)

    def send_y(d, carry):
        to = my_z * y_count + lax.rem(my_y + d, y_count)
        pltpu.make_async_remote_copy(
            src_ref=row_taps.at[my_y],
            dst_ref=row_taps.at[my_y],
            send_sem=send_sems.at[0],
            recv_sem=recv_sems.at[0],
            device_id={"seq": to},
            device_id_type=MESH,
        ).start()
        return carry

    lax.fori_loop(1, y_count, send_y, 0)

    def send_first(d, carry):
        to = partner(d)
        pltpu.make_async_remote_copy(
            src_ref=send1.at[to],
            dst_ref=recv1.at[me],
            send_sem=send_sems.at[1],
            recv_sem=recv_sems.at[1],
            device_id={"seq": to},
            device_id_type=MESH,
        ).start()
        return carry

    lax.fori_loop(1, seq_count, send_first, 0)
    recv1[me] = send1[me]

    def wait_all(ref, sem):
        pltpu.make_async_copy(ref, ref, sem).wait()

    wait_all(row_taps.at[pl.ds(0, y_count - 1)], recv_sems.at[0])

    def send_z(d, carry):
        to = lax.rem(my_z + d, z_count) * y_count + my_y
        pltpu.make_async_remote_copy(
            src_ref=row_taps,
            dst_ref=all_taps.at[pl.ds(my_z * y_count, y_count)],
            send_sem=send_sems.at[2],
            recv_sem=recv_sems.at[2],
            device_id={"seq": to},
            device_id_type=MESH,
        ).start()
        return carry

    lax.fori_loop(1, z_count, send_z, 0)
    all_taps[pl.ds(my_z * y_count, y_count)] = row_taps[...]
    wait_all(all_taps.at[pl.ds(0, (z_count - 1) * y_count)], recv_sems.at[2])

    filters = taps_ref.shape[0]
    for f in range(filters):

        def build(o, before):
            row = jnp.broadcast_to(all_taps[o, f : f + 1, :], (LANES, LANES))
            now = pltpu.roll(row, 1, 1, stride=1, stride_axis=0)
            block = jnp.where(lane_id > row_id, before, now)
            toeplitz[f, pl.ds(pl.multiple_of(o * LANES, LANES), LANES), :] = block.astype(bf16)
            return now

        lax.fori_loop(0, blocks, build, jnp.zeros((LANES, LANES), f32))

    wait_all(recv1.at[pl.ds(0, seq_count - 1)], recv_sems.at[1])

    halves = 2 * blocks
    slot = lax.broadcasted_iota(jnp.int32, (halves, halves), 0)
    column = lax.broadcasted_iota(jnp.int32, (halves, halves), 1)
    split = (2 * lax.rem(column, blocks) + lax.div(column, blocks) == slot).astype(bf16)
    ids = ids_ref[...].reshape(1, halves).astype(f32).astype(bf16)
    split_ids = jnp.dot(ids, split, preferred_element_type=f32).astype(jnp.int32)
    half = 2 * lax.rem(slot, blocks) + lax.div(slot, blocks)
    place = jnp.where(half == split_ids, 1.0, 0.0)

    low_lane = lax.broadcasted_iota(jnp.int32, (blocks, LANES), 1) < HALF

    def doubled(rows):
        other = pltpu.roll(rows, HALF, 1)
        return jnp.concatenate(
            [jnp.where(low_lane, rows, other), jnp.where(low_lane, other, rows)], axis=0
        ).astype(bf16)

    def joined(rows):
        return jnp.where(low_lane, rows[0:blocks], rows[blocks : 2 * blocks])

    wide1[...] = recv1[...].astype(f32).reshape(blocks * 16, LANES)
    sorter = place.astype(bf16)
    for c in range(16):
        rows = doubled(wide1[pl.ds(c, blocks, stride=16), :])
        rows = joined(jnp.dot(sorter, rows, preferred_element_type=f32))
        a, f = (c % 8) // filters, c % filters
        target = grad_rows if c < 8 else value_rows
        target[f, pl.ds(a, blocks, stride=2), :] = rows
    for f in range(filters):
        grad_rows[f, pl.ds(live, 2 * SPAN), :] = jnp.zeros((2 * SPAN, LANES), f32)

    for f in range(filters):
        for o in range(SPAN):
            hankel[f, pl.ds(0, live), pl.ds(o * LANES, LANES)] = grad_rows[
                f, pl.ds(2 * o, live), :
            ].astype(bf16)
        hankel[f, pl.ds(live, live), :] = jnp.zeros((live, SPAN * LANES), bf16)

        turned = lax.dot_general(
            flip,
            value_rows[f].astype(bf16),
            (((1,), (1,)), ((), ())),
            preferred_element_type=f32,
        ).astype(bf16)

        def contract(p, total):
            rows = pl.ds(pl.multiple_of(p * 2 * SPAN, 2 * SPAN), live)
            wide = pl.ds(pl.multiple_of(p * SPAN * LANES, SPAN * LANES), SPAN * LANES)
            panel = hankel[f, rows, :]
            lag_mat[:, wide] = jnp.dot(turned, panel, preferred_element_type=f32)
            return total + jnp.dot(panel, toeplitz[f, wide, :], preferred_element_type=f32)

        total = lax.fori_loop(0, panels, contract, jnp.zeros((live, LANES), f32))
        out_rows[f] = total * norm_scale
        lag_mat[:, pl.ds(blocks * LANES, LANES)] = jnp.zeros((LANES, LANES), f32)

        def skew(o, carry):
            here = lag_mat[:, pl.ds(pl.multiple_of(o * LANES, LANES), LANES)]
            after = lag_mat[:, pl.ds(pl.multiple_of((o + 1) * LANES, LANES), LANES)]
            chosen = jnp.where(row_id + lane_id >= LANES - 1, here, after)
            rolled = pltpu.roll(chosen, 1, 1, stride=1, stride_axis=0)
            row = jnp.sum(rolled, axis=0, keepdims=True) * norm_scale
            rounded = row.astype(bf16).astype(f32)
            wide2[pl.ds(o * 16 + 8 + f, 1), :] = rounded
            wide2[pl.ds(o * 16 + 12 + f, 1), :] = row - rounded
            return carry

        lax.fori_loop(0, blocks, skew, 0)

    unsorter = place.T.astype(bf16)
    for c in range(8):
        rows = doubled(out_rows[c % filters, pl.ds(c // filters, blocks, stride=2), :])
        rows = joined(jnp.dot(unsorter, rows, preferred_element_type=f32))
        wide2[pl.ds(c, blocks, stride=16), :] = rows
    send2[...] = wide2[...].reshape(blocks, 16, LANES).astype(bf16)

    def send_back(d, carry):
        to = partner(d)
        pltpu.make_async_remote_copy(
            src_ref=send2.at[to],
            dst_ref=recv2.at[me],
            send_sem=send_sems.at[3],
            recv_sem=recv_sems.at[3],
            device_id={"seq": to},
            device_id_type=MESH,
        ).start()
        return carry

    lax.fori_loop(1, seq_count, send_back, 0)
    recv2[me] = send2[me]
    wait_all(recv2.at[pl.ds(0, seq_count - 1)], recv_sems.at[3])

    def add_lags(p, total):
        return total + recv2[p].astype(f32)

    summed = lax.fori_loop(0, seq_count, add_lags, jnp.zeros((16, LANES), f32))
    part[...] = summed[8:16]

    def send_ch(d, carry):
        pltpu.make_async_remote_copy(
            src_ref=part,
            dst_ref=parts.at[my_ch],
            send_sem=send_sems.at[4],
            recv_sem=recv_sems.at[4],
            device_id={"ch": lax.rem(my_ch + d, ch_count)},
            device_id_type=MESH,
        ).start()
        return carry

    lax.fori_loop(1, ch_count, send_ch, 0)
    parts[my_ch] = part[...]

    for c in range(vg_ref.shape[1] // LANES):
        group = LANES // 8
        rows = recv2[pl.ds(c * group, group)].astype(f32)[:, 0:8, :].reshape(LANES, LANES)
        vg_ref[:, pl.ds(c * LANES, LANES)] = rows.T.astype(bf16)

    wait_all(parts.at[pl.ds(0, ch_count - 1)], recv_sems.at[4])
    both = jnp.sum(parts[...], axis=0)
    fg_ref[...] = both[0:filters] + both[filters : 2 * filters]

    wait_all(row_taps.at[pl.ds(0, y_count - 1)], send_sems.at[0])
    wait_all(send1.at[pl.ds(0, seq_count - 1)], send_sems.at[1])
    wait_all(all_taps.at[pl.ds(0, (z_count - 1) * y_count)], send_sems.at[2])
    wait_all(send2.at[pl.ds(0, seq_count - 1)], send_sems.at[3])
    wait_all(parts.at[pl.ds(0, ch_count - 1)], send_sems.at[4])


def local(upstream_grad, gate_act, value_act, filter_taps, half_ids):
    seq_count = lax.axis_size("seq")
    ch_count = lax.axis_size("ch")
    local_rows, channels = upstream_grad.shape
    filters = filter_taps.shape[0]
    blocks = seq_count
    y_count = 1 << ((seq_count.bit_length() - 1) // 2)
    f32, bf16 = jnp.float32, jnp.bfloat16
    vmem = pl.BlockSpec(memory_space=pltpu.VMEM)
    return pl.pallas_call(
        functools.partial(kernel, seq_count, ch_count),
        out_shape=(
            jax.ShapeDtypeStruct((local_rows, channels), bf16),
            jax.ShapeDtypeStruct((filters, LANES), f32),
        ),
        in_specs=[vmem] * 5,
        out_specs=(vmem, vmem),
        scratch_shapes=[
            pltpu.VMEM((y_count, filters, LANES), f32),
            pltpu.VMEM((blocks, filters, LANES), f32),
            pltpu.VMEM((seq_count, 16, LANES), bf16),
            pltpu.VMEM((seq_count, 16, LANES), bf16),
            pltpu.VMEM((blocks * 16, LANES), f32),
            pltpu.VMEM((filters, 2 * (blocks + SPAN), LANES), f32),
            pltpu.VMEM((filters, 2 * blocks, LANES), f32),
            pltpu.VMEM((filters, blocks * LANES, LANES), bf16),
            pltpu.VMEM((filters, 4 * blocks, SPAN * LANES), bf16),
            pltpu.VMEM((LANES, (blocks + 1) * LANES), f32),
            pltpu.VMEM((filters, 2 * blocks, LANES), f32),
            pltpu.VMEM((blocks * 16, LANES), f32),
            pltpu.VMEM((seq_count, 16, LANES), bf16),
            pltpu.VMEM((seq_count, 16, LANES), bf16),
            pltpu.VMEM((8, LANES), f32),
            pltpu.VMEM((ch_count, 8, LANES), f32),
            pltpu.SemaphoreType.DMA((5,)),
            pltpu.SemaphoreType.DMA((5,)),
        ],
        compiler_params=pltpu.CompilerParams(
            collective_id=0, has_side_effects=True, vmem_limit_bytes=40 * 1024 * 1024
        ),
        cost_estimate=pl.CostEstimate(
            flops=4 * 8 * (blocks * LANES) ** 2,
            bytes_accessed=4 * local_rows * channels * 2,
            transcendentals=0,
        ),
    )(upstream_grad, gate_act, value_act, filter_taps, half_ids)


def solution(mesh):
    placed = (P("seq", "ch"), P("seq", "ch"), P("seq", "ch"), P(None, "seq"), P())
    return jax.shard_map(
        local,
        mesh=mesh,
        in_specs=placed,
        out_specs=(P("seq", "ch"), P(None, "seq")),
        check_vma=False,
    )
```

```python
import functools
import math

import jax
import jax.numpy as jnp
import ml_dtypes
import numpy as np
from jax import lax
from jax.experimental import pallas as pl
from jax.experimental.pallas import tpu as pltpu
from jax.sharding import PartitionSpec as P

MESH = pl.DeviceIdType.MESH
LANES = 128
HALF = 64


def two_parts(table):
    high = table.astype(ml_dtypes.bfloat16)
    rest = (table - high.astype(np.float64)).astype(ml_dtypes.bfloat16)
    return high, rest


@functools.lru_cache(maxsize=None)
def tables(halves):
    tall = 2 * halves
    points = tall * HALF
    angle = 2 * np.pi * np.outer(np.arange(tall), np.arange(halves)) / tall
    cosine, sine = np.cos(angle), -np.sin(angle)
    parts = two_parts(cosine) + two_parts(sine)
    forward = np.concatenate(parts, 0)
    back = np.ascontiguousarray(np.concatenate(parts, 0).T)
    natural = np.concatenate([np.arange(0, halves, 2), np.arange(1, halves, 2)])
    both = np.concatenate([cosine, sine], 0)[:, natural]
    taps = np.concatenate(two_parts(both), 1)
    lags = np.stack(two_parts(np.ascontiguousarray(both.T)))
    turn = 2 * np.pi * np.outer(np.arange(tall), np.arange(HALF)) / points
    turn = np.tile(turn, (1, 2))
    twiddle = np.stack([np.cos(turn), -np.sin(turn)]).astype(np.float32)
    small = 2 * np.pi * np.outer(np.arange(HALF), np.arange(HALF)) / HALF
    pair = np.eye(2)
    real, imag = np.kron(pair, np.cos(small)), np.kron(pair, -np.sin(small))
    inner = np.stack(two_parts(np.block([[real, imag], [-imag, real]])))
    outer = np.stack(two_parts(np.block([[real, -imag], [imag, real]])))
    return forward, back, taps, lags, twiddle, inner, outer


def kernel(
    seq_count,
    ch_count,
    up_hbm,
    gate_hbm,
    value_hbm,
    taps_hbm,
    ids_hbm,
    forward_hbm,
    back_hbm,
    taps_tab_hbm,
    lags_hbm,
    twiddle_hbm,
    inner_hbm,
    outer_hbm,
    vg_ref,
    fg_ref,
    up_ref,
    gate_ref,
    value_ref,
    taps_ref,
    ids_ref,
    forward,
    back,
    taps_tab,
    lags_tab,
    twiddle,
    inner,
    outer,
    row_taps,
    packed_taps,
    all_taps,
    send1,
    recv1,
    wide1,
    left,
    left_back,
    spectra,
    wide2,
    send2,
    recv2,
    part,
    parts,
    load_sems,
    send_sems,
    recv_sems,
):
    f32, bf16 = jnp.float32, jnp.bfloat16
    y_count = 1 << ((seq_count.bit_length() - 1) // 2)
    z_count = seq_count // y_count
    me = lax.axis_index("seq")
    my_ch = lax.axis_index("ch")
    my_z, my_y = lax.div(me, y_count), lax.rem(me, y_count)
    blocks = seq_count
    halves = 2 * blocks
    tall = 2 * halves
    filters = taps_ref.shape[0]
    scale = 1.0 / math.sqrt(blocks * LANES) / (tall * HALF)

    pairs = (
        (up_hbm, up_ref),
        (gate_hbm, gate_ref),
        (value_hbm, value_ref),
        (taps_hbm, taps_ref),
        (ids_hbm, ids_ref),
        (forward_hbm, forward),
        (back_hbm, back),
        (taps_tab_hbm, taps_tab),
        (lags_hbm, lags_tab),
        (twiddle_hbm, twiddle),
        (inner_hbm, inner),
        (outer_hbm, outer),
    )
    loads = [
        pltpu.make_async_copy(src, dst, load_sems.at[i]) for i, (src, dst) in enumerate(pairs)
    ]
    for load in loads:
        load.start()

    def partner(d):
        z = lax.rem(my_z + lax.div(d, y_count), z_count)
        y = lax.rem(my_y + lax.rem(d, y_count), y_count)
        return z * y_count + y

    barrier = pltpu.get_barrier_semaphore()

    def greet(d, carry):
        pl.semaphore_signal(barrier, inc=1, device_id={"seq": partner(d)}, device_id_type=MESH)
        return carry

    lax.fori_loop(1, seq_count, greet, 0)

    def greet_ch(d, carry):
        pl.semaphore_signal(
            barrier, inc=1, device_id={"ch": lax.rem(my_ch + d, ch_count)}, device_id_type=MESH
        )
        return carry

    lax.fori_loop(1, ch_count, greet_ch, 0)

    for load in loads[0:4]:
        load.wait()
    own = taps_ref[...].astype(f32)
    row_taps[pl.ds(pl.multiple_of(my_y * 8, 8), 8), :] = jnp.concatenate([own, own], axis=0)

    group = LANES // 8
    for c in range(up_ref.shape[1] // LANES):
        cols = pl.ds(c * LANES, LANES)
        product = up_ref[:, cols].astype(f32) * gate_ref[:, cols].astype(f32)
        value = value_ref[:, cols].astype(f32)
        send1[pl.ds(c * group, group)] = jnp.concatenate(
            [product.T.reshape(group, 8, LANES), value.T.reshape(group, 8, LANES)], axis=1
        ).astype(bf16)

    pl.semaphore_wait(barrier, seq_count - 1 + ch_count - 1)

    def send_y(d, carry):
        mine = row_taps.at[pl.ds(pl.multiple_of(my_y * 8, 8), 8)]
        pltpu.make_async_remote_copy(
            src_ref=mine,
            dst_ref=mine,
            send_sem=send_sems.at[0],
            recv_sem=recv_sems.at[0],
            device_id={"seq": my_z * y_count + lax.rem(my_y + d, y_count)},
            device_id_type=MESH,
        ).start()
        return carry

    lax.fori_loop(1, y_count, send_y, 0)

    def send_first(d, carry):
        to = partner(d)
        pltpu.make_async_remote_copy(
            src_ref=send1.at[to],
            dst_ref=recv1.at[me],
            send_sem=send_sems.at[1],
            recv_sem=recv_sems.at[1],
            device_id={"seq": to},
            device_id_type=MESH,
        ).start()
        return carry

    lax.fori_loop(1, seq_count, send_first, 0)
    recv1[me] = send1[me]

    def wait_all(ref, sem):
        pltpu.make_async_copy(ref, ref, sem).wait()

    wait_all(row_taps.at[pl.ds(0, (y_count - 1) * 8)], recv_sems.at[0])

    packed_taps[...] = jnp.concatenate(
        [row_taps[pl.ds(f, y_count, stride=8), :] for f in range(filters)], axis=0
    ).astype(bf16)

    def send_z(d, carry):
        pltpu.make_async_remote_copy(
            src_ref=packed_taps,
            dst_ref=all_taps.at[my_z],
            send_sem=send_sems.at[2],
            recv_sem=recv_sems.at[2],
            device_id={"seq": lax.rem(my_z + d, z_count) * y_count + my_y},
            device_id_type=MESH,
        ).start()
        return carry

    lax.fori_loop(1, z_count, send_z, 0)
    all_taps[my_z] = packed_taps[...]

    for load in loads[4:]:
        load.wait()
    slot = lax.broadcasted_iota(jnp.int32, (halves, halves), 0)
    column = lax.broadcasted_iota(jnp.int32, (halves, halves), 1)
    split = (2 * lax.rem(column, blocks) + lax.div(column, blocks) == slot).astype(bf16)
    ids = ids_ref[...].reshape(1, halves).astype(f32).astype(bf16)
    split_ids = jnp.dot(ids, split, preferred_element_type=f32).astype(jnp.int32)
    place = jnp.where(slot == split_ids, 1.0, 0.0)
    sorted_cols = jnp.dot(forward[...], place.astype(bf16), preferred_element_type=f32)
    sorted_rows = jnp.dot(place.T.astype(bf16), back[...], preferred_element_type=f32)
    for n in range(2):
        cosine, sine = sorted_cols[n * tall : (n + 1) * tall], sorted_cols[(n + 2) * tall : (n + 3) * tall]
        left[0:tall, n * tall : (n + 1) * tall] = jnp.concatenate([cosine, -sine], axis=1).astype(bf16)
        left[tall : 2 * tall, n * tall : (n + 1) * tall] = jnp.concatenate([sine, cosine], axis=1).astype(
            bf16
        )
        cosine = sorted_rows[:, n * tall : (n + 1) * tall]
        sine = sorted_rows[:, (n + 2) * tall : (n + 3) * tall]
        left_back[n, 0:halves, :] = jnp.concatenate([cosine, sine], axis=1).astype(bf16)
        left_back[n, halves : 2 * halves, :] = jnp.concatenate([-sine, cosine], axis=1).astype(bf16)

    low_lane = lax.broadcasted_iota(jnp.int32, (blocks, LANES), 1) < HALF

    def by_halves(rows0, rows1):
        return jnp.concatenate(
            [
                jnp.where(low_lane, rows0, pltpu.roll(rows1, HALF, 1)),
                jnp.where(low_lane, pltpu.roll(rows0, HALF, 1), rows1),
            ],
            axis=0,
        )

    def joined(rows):
        even, odd = rows[0:blocks], rows[blocks : 2 * blocks]
        return (
            jnp.where(low_lane, even, pltpu.roll(odd, HALF, 1)),
            jnp.where(low_lane, pltpu.roll(even, HALF, 1), odd),
        )

    def parts_of(x):
        high = x.astype(bf16)
        return high, (x - high.astype(f32)).astype(bf16)

    def dot(a, b):
        return jnp.dot(a, b, preferred_element_type=f32)

    def product_right(x, table):
        high, rest = parts_of(x)
        return dot(high, table[0]) + dot(high, table[1]) + dot(rest, table[0])

    def product_left(table, x):
        high, rest = parts_of(x)
        return dot(table[0], high) + dot(table[1], high) + dot(table[0], rest)

    def spectrum(re, im):
        cosine, sine = twiddle[0], twiddle[1]
        turned = jnp.concatenate([re * cosine - im * sine, re * sine + im * cosine], axis=1)
        return product_right(turned, inner)

    def conj_times(a, b):
        ar, ai = a[:, 0:LANES], a[:, LANES:]
        br, bi = b[:, 0:LANES], b[:, LANES:]
        return jnp.concatenate([ar * br + ai * bi, ar * bi - ai * br], axis=1)

    def unturned(x):
        y = product_right(x, outer)
        re, im = y[:, 0:LANES], y[:, LANES:]
        cosine, sine = twiddle[0], twiddle[1]
        return jnp.concatenate([re * cosine + im * sine, im * cosine - re * sine], axis=0)

    wait_all(all_taps.at[pl.ds(0, z_count - 1)], recv_sems.at[2])
    taps_wide = all_taps[...].astype(f32)

    def taps_of(f):
        return taps_wide[:, f * y_count : (f + 1) * y_count, :].reshape(blocks, LANES)

    taps_in = jnp.concatenate(
        [by_halves(taps_of(f), taps_of(f + 1)) for f in range(0, filters, 2)], axis=1
    ).astype(bf16)
    taps_first = dot(taps_tab[...], jnp.concatenate([taps_in, taps_in], axis=0))
    for q in range(filters // 2):
        lanes = slice(q * LANES, (q + 1) * LANES)
        spectra[q] = spectrum(taps_first[0:tall, lanes], taps_first[tall:, lanes])

    wait_all(recv1.at[pl.ds(0, seq_count - 1)], recv_sems.at[1])
    wide1[...] = recv1[...].astype(f32).reshape(blocks * 16, LANES)

    def first_stage(base):
        columns = []
        for f in range(0, filters, 2):
            rows = [
                by_halves(
                    wide1[pl.ds(base + a * filters + f, blocks, stride=16), :],
                    wide1[pl.ds(base + a * filters + f + 1, blocks, stride=16), :],
                )
                for a in range(2)
            ]
            columns.append(jnp.concatenate(rows, axis=0))
        data = jnp.concatenate(columns, axis=1).astype(bf16)
        return dot(left[...], jnp.concatenate([data, data], axis=0))

    grad_first = first_stage(0)
    value_first = first_stage(8)
    grad_back, lag_back = [], []
    for q in range(filters // 2):
        lanes = slice(q * LANES, (q + 1) * LANES)
        grad_spec = spectrum(grad_first[0:tall, lanes], grad_first[tall:, lanes])
        value_spec = spectrum(value_first[0:tall, lanes], value_first[tall:, lanes])
        grad_back.append(unturned(conj_times(spectra[q], grad_spec)))
        lag_back.append(unturned(conj_times(value_spec, grad_spec)))
    in_grad = product_left(left_back, jnp.concatenate(grad_back, axis=1)) * scale
    lag_sums = product_left(lags_tab, jnp.concatenate(lag_back, axis=1)) * scale

    for q in range(filters // 2):
        lanes = slice(q * LANES, (q + 1) * LANES)
        for a in range(2):
            for n, rows in enumerate(joined(in_grad[a * halves : (a + 1) * halves, lanes])):
                wide2[pl.ds(a * filters + 2 * q + n, blocks, stride=16), :] = rows
        for n, rows in enumerate(joined(lag_sums[:, lanes])):
            rounded = rows.astype(bf16).astype(f32)
            wide2[pl.ds(8 + 2 * q + n, blocks, stride=16), :] = rounded
            wide2[pl.ds(8 + filters + 2 * q + n, blocks, stride=16), :] = rows - rounded
    send2[...] = wide2[...].reshape(blocks, 16, LANES).astype(bf16)

    def send_back(d, carry):
        to = partner(d)
        pltpu.make_async_remote_copy(
            src_ref=send2.at[to],
            dst_ref=recv2.at[me],
            send_sem=send_sems.at[3],
            recv_sem=recv_sems.at[3],
            device_id={"seq": to},
            device_id_type=MESH,
        ).start()
        return carry

    lax.fori_loop(1, seq_count, send_back, 0)
    recv2[me] = send2[me]
    wait_all(recv2.at[pl.ds(0, seq_count - 1)], recv_sems.at[3])

    def add_lags(p, total):
        return total + recv2[p].astype(f32)

    summed = lax.fori_loop(0, seq_count, add_lags, jnp.zeros((16, LANES), f32))
    part[...] = summed[8:16]

    def send_ch(d, carry):
        pltpu.make_async_remote_copy(
            src_ref=part,
            dst_ref=parts.at[my_ch],
            send_sem=send_sems.at[4],
            recv_sem=recv_sems.at[4],
            device_id={"ch": lax.rem(my_ch + d, ch_count)},
            device_id_type=MESH,
        ).start()
        return carry

    lax.fori_loop(1, ch_count, send_ch, 0)
    parts[my_ch] = part[...]

    for c in range(vg_ref.shape[1] // LANES):
        rows = recv2[pl.ds(c * group, group)].astype(f32)[:, 0:8, :].reshape(LANES, LANES)
        vg_ref[:, pl.ds(c * LANES, LANES)] = rows.T.astype(bf16)

    wait_all(parts.at[pl.ds(0, ch_count - 1)], recv_sems.at[4])
    both = jnp.sum(parts[...], axis=0)
    fg_ref[...] = both[0:filters] + both[filters : 2 * filters]

    wait_all(row_taps.at[pl.ds(0, (y_count - 1) * 8)], send_sems.at[0])
    wait_all(send1.at[pl.ds(0, seq_count - 1)], send_sems.at[1])
    wait_all(all_taps.at[pl.ds(0, z_count - 1)], send_sems.at[2])
    wait_all(send2.at[pl.ds(0, seq_count - 1)], send_sems.at[3])
    wait_all(parts.at[pl.ds(0, ch_count - 1)], send_sems.at[4])


def local(upstream_grad, gate_act, value_act, filter_taps, half_ids):
    seq_count = lax.axis_size("seq")
    ch_count = lax.axis_size("ch")
    local_rows, channels = upstream_grad.shape
    filters = filter_taps.shape[0]
    blocks = seq_count
    halves = 2 * blocks
    tall = 2 * halves
    y_count = 1 << ((seq_count.bit_length() - 1) // 2)
    f32, bf16 = jnp.float32, jnp.bfloat16
    constants = [jnp.asarray(table) for table in tables(halves)]
    vmem = pl.BlockSpec(memory_space=pltpu.VMEM)
    operands = [upstream_grad, gate_act, value_act, filter_taps, half_ids] + constants
    return pl.pallas_call(
        functools.partial(kernel, seq_count, ch_count),
        out_shape=(
            jax.ShapeDtypeStruct((local_rows, channels), bf16),
            jax.ShapeDtypeStruct((filters, LANES), f32),
        ),
        in_specs=[pl.BlockSpec(memory_space=pl.ANY)] * len(operands),
        out_specs=(vmem, vmem),
        scratch_shapes=[pltpu.VMEM(x.shape, x.dtype) for x in operands]
        + [
            pltpu.VMEM((y_count * 8, LANES), f32),
            pltpu.VMEM((filters * y_count, LANES), bf16),
            pltpu.VMEM((seq_count // y_count, filters * y_count, LANES), bf16),
            pltpu.VMEM((seq_count, 16, LANES), bf16),
            pltpu.VMEM((seq_count, 16, LANES), bf16),
            pltpu.VMEM((blocks * 16, LANES), f32),
            pltpu.VMEM((2 * tall, 2 * tall), bf16),
            pltpu.VMEM((2, 2 * halves, 2 * tall), bf16),
            pltpu.VMEM((filters // 2, tall, 2 * LANES), f32),
            pltpu.VMEM((blocks * 16, LANES), f32),
            pltpu.VMEM((seq_count, 16, LANES), bf16),
            pltpu.VMEM((seq_count, 16, LANES), bf16),
            pltpu.VMEM((8, LANES), f32),
            pltpu.VMEM((ch_count, 8, LANES), f32),
            pltpu.SemaphoreType.DMA((len(operands),)),
            pltpu.SemaphoreType.DMA((5,)),
            pltpu.SemaphoreType.DMA((5,)),
        ],
        compiler_params=pltpu.CompilerParams(
            collective_id=0, has_side_effects=True, vmem_limit_bytes=40 * 1024 * 1024
        ),
        cost_estimate=pl.CostEstimate(
            flops=40 * 2 * 256**3,
            bytes_accessed=4 * local_rows * channels * 2,
            transcendentals=0,
        ),
    )(*operands)


def solution(mesh):
    placed = (P("seq", "ch"), P("seq", "ch"), P("seq", "ch"), P(None, "seq"), P())
    return jax.shard_map(
        local,
        mesh=mesh,
        in_specs=placed,
        out_specs=(P("seq", "ch"), P(None, "seq")),
        check_vma=False,
    )
```

```python
import functools
import math

import jax
import jax.numpy as jnp
import ml_dtypes
import numpy as np
from jax import lax
from jax.experimental import pallas as pl
from jax.experimental.pallas import tpu as pltpu
from jax.sharding import PartitionSpec as P

MESH = pl.DeviceIdType.MESH
LANES = 128
HALF = 64


def two_parts(table):
    high = table.astype(ml_dtypes.bfloat16)
    rest = (table - high.astype(np.float64)).astype(ml_dtypes.bfloat16)
    return high, rest


@functools.lru_cache(maxsize=None)
def tables(halves):
    tall = 2 * halves
    points = tall * HALF
    angle = 2 * np.pi * np.outer(np.arange(tall), np.arange(halves)) / tall
    cosine, sine = np.cos(angle), -np.sin(angle)
    parts = two_parts(cosine) + two_parts(sine)
    forward = np.concatenate([np.concatenate(parts[0:2], 0), np.concatenate(parts[2:4], 0)], 1)
    back = np.concatenate([part.T for part in parts], 0)
    natural = np.concatenate([np.arange(0, halves, 2), np.arange(1, halves, 2)])
    both = np.concatenate([cosine, sine], 0)[:, natural]
    taps = np.concatenate(two_parts(both), 1)
    lags = np.concatenate(two_parts(cosine.T[natural]) + two_parts(sine.T[natural]), 0)
    turn = 2 * np.pi * np.outer(np.arange(tall), np.arange(HALF)) / points
    turn = np.tile(turn, (1, 2))
    twiddle = np.stack([np.cos(turn), -np.sin(turn)]).astype(np.float32)
    small = 2 * np.pi * np.outer(np.arange(HALF), np.arange(HALF)) / HALF
    pair = np.eye(2)
    real, imag = np.kron(pair, np.cos(small)), np.kron(pair, -np.sin(small))
    inner = two_parts(np.block([[real, imag], [-imag, real]]))
    outer = two_parts(np.block([[real, -imag], [imag, real]]))
    return twiddle, (forward, back, taps, lags) + inner + outer


def kernel(
    seq_count,
    ch_count,
    up_hbm,
    gate_hbm,
    value_hbm,
    taps_hbm,
    ids_hbm,
    twiddle_hbm,
    matrix_hbm,
    vg_ref,
    fg_ref,
    up_ref,
    gate_ref,
    value_ref,
    taps_ref,
    ids_ref,
    twiddle,
    matrix,
    row_taps,
    packed_taps,
    all_taps,
    send1,
    recv1,
    wide1,
    left,
    left_back,
    spectra,
    wide2,
    send2,
    recv2,
    part,
    parts,
    load_sems,
    send_sems,
    recv_sems,
):
    f32, bf16 = jnp.float32, jnp.bfloat16
    y_count = 1 << ((seq_count.bit_length() - 1) // 2)
    z_count = seq_count // y_count
    me = lax.axis_index("seq")
    my_ch = lax.axis_index("ch")
    my_z, my_y = lax.div(me, y_count), lax.rem(me, y_count)
    blocks = seq_count
    halves = 2 * blocks
    tall = 2 * halves
    filters = taps_ref.shape[0]
    scale = 1.0 / math.sqrt(blocks * LANES) / (tall * HALF)

    pairs = (
        (up_hbm, up_ref),
        (gate_hbm, gate_ref),
        (value_hbm, value_ref),
        (taps_hbm, taps_ref),
        (ids_hbm, ids_ref),
        (twiddle_hbm, twiddle),
        (matrix_hbm, matrix),
    )
    loads = [
        pltpu.make_async_copy(src, dst, load_sems.at[i]) for i, (src, dst) in enumerate(pairs)
    ]
    for load in loads:
        load.start()

    def partner(d):
        z = lax.rem(my_z + lax.div(d, y_count), z_count)
        y = lax.rem(my_y + lax.rem(d, y_count), y_count)
        return z * y_count + y

    barrier = pltpu.get_barrier_semaphore()

    def greet(d, carry):
        pl.semaphore_signal(barrier, inc=1, device_id={"seq": partner(d)}, device_id_type=MESH)
        return carry

    lax.fori_loop(1, seq_count, greet, 0)

    def greet_ch(d, carry):
        pl.semaphore_signal(
            barrier, inc=1, device_id={"ch": lax.rem(my_ch + d, ch_count)}, device_id_type=MESH
        )
        return carry

    lax.fori_loop(1, ch_count, greet_ch, 0)

    for load in loads[0:4]:
        load.wait()
    own = taps_ref[...].astype(f32)
    row_taps[pl.ds(pl.multiple_of(my_y * 8, 8), 8), :] = jnp.concatenate([own, own], axis=0)

    group = LANES // 8
    for c in range(up_ref.shape[1] // LANES):
        cols = pl.ds(c * LANES, LANES)
        product = up_ref[:, cols].astype(f32) * gate_ref[:, cols].astype(f32)
        value = value_ref[:, cols].astype(f32)
        send1[pl.ds(c * group, group)] = jnp.concatenate(
            [product.T.reshape(group, 8, LANES), value.T.reshape(group, 8, LANES)], axis=1
        ).astype(bf16)

    pl.semaphore_wait(barrier, seq_count - 1 + ch_count - 1)

    def send_y(d, carry):
        mine = row_taps.at[pl.ds(pl.multiple_of(my_y * 8, 8), 8)]
        pltpu.make_async_remote_copy(
            src_ref=mine,
            dst_ref=mine,
            send_sem=send_sems.at[0],
            recv_sem=recv_sems.at[0],
            device_id={"seq": my_z * y_count + lax.rem(my_y + d, y_count)},
            device_id_type=MESH,
        ).start()
        return carry

    lax.fori_loop(1, y_count, send_y, 0)

    def send_first(d, carry):
        to = partner(d)
        pltpu.make_async_remote_copy(
            src_ref=send1.at[to],
            dst_ref=recv1.at[me],
            send_sem=send_sems.at[1],
            recv_sem=recv_sems.at[1],
            device_id={"seq": to},
            device_id_type=MESH,
        ).start()
        return carry

    lax.fori_loop(1, seq_count, send_first, 0)
    recv1[me] = send1[me]

    def wait_all(ref, sem):
        pltpu.make_async_copy(ref, ref, sem).wait()

    wait_all(row_taps.at[pl.ds(0, (y_count - 1) * 8)], recv_sems.at[0])

    packed_taps[...] = jnp.concatenate(
        [row_taps[pl.ds(f, y_count, stride=8), :] for f in range(filters)], axis=0
    ).astype(bf16)

    def send_z(d, carry):
        pltpu.make_async_remote_copy(
            src_ref=packed_taps,
            dst_ref=all_taps.at[my_z],
            send_sem=send_sems.at[2],
            recv_sem=recv_sems.at[2],
            device_id={"seq": lax.rem(my_z + d, z_count) * y_count + my_y},
            device_id_type=MESH,
        ).start()
        return carry

    lax.fori_loop(1, z_count, send_z, 0)
    all_taps[my_z] = packed_taps[...]

    for load in loads[4:]:
        load.wait()
    slot = lax.broadcasted_iota(jnp.int32, (halves, halves), 0)
    column = lax.broadcasted_iota(jnp.int32, (halves, halves), 1)
    split = (2 * lax.rem(column, blocks) + lax.div(column, blocks) == slot).astype(bf16)
    ids = ids_ref[...].reshape(1, halves).astype(f32).astype(bf16)
    split_ids = jnp.dot(ids, split, preferred_element_type=f32).astype(jnp.int32)
    place = jnp.where(slot == split_ids, 1.0, 0.0)
    chooser, chooser_rows = place.astype(bf16), place.T.astype(bf16)

    def table(start, rows, first=0, columns=tall):
        return matrix[start : start + rows, first : first + columns]

    for n in range(2):
        cosine = jnp.dot(table(n * tall, tall, 0, halves), chooser, preferred_element_type=f32)
        sine = jnp.dot(table(n * tall, tall, halves, halves), chooser, preferred_element_type=f32)
        left[0:tall, n * tall : (n + 1) * tall] = jnp.concatenate([cosine, -sine], axis=1).astype(bf16)
        left[tall : 2 * tall, n * tall : (n + 1) * tall] = jnp.concatenate([sine, cosine], axis=1).astype(
            bf16
        )
        start = 2 * tall + n * halves
        cosine = jnp.dot(chooser_rows, table(start, halves), preferred_element_type=f32)
        sine = jnp.dot(chooser_rows, table(start + tall, halves), preferred_element_type=f32)
        left_back[n, 0:halves, :] = jnp.concatenate([cosine, sine], axis=1).astype(bf16)
        left_back[n, halves : 2 * halves, :] = jnp.concatenate([-sine, cosine], axis=1).astype(bf16)

    taps_tab = table(4 * tall, 2 * tall)
    start = 6 * tall
    lags_tab = [
        jnp.concatenate(
            [table(start + n * halves, halves), table(start + tall + n * halves, halves)], axis=1
        )
        for n in range(2)
    ]
    inner_rows, outer_rows = 8 * tall, 8 * tall + 4 * LANES
    inner = [table(inner_rows + n * 2 * LANES, 2 * LANES, 0, 2 * LANES) for n in range(2)]
    outer = [table(outer_rows + n * 2 * LANES, 2 * LANES, 0, 2 * LANES) for n in range(2)]

    low_lane = lax.broadcasted_iota(jnp.int32, (blocks, LANES), 1) < HALF

    def by_halves(rows0, rows1):
        return jnp.concatenate(
            [
                jnp.where(low_lane, rows0, pltpu.roll(rows1, HALF, 1)),
                jnp.where(low_lane, pltpu.roll(rows0, HALF, 1), rows1),
            ],
            axis=0,
        )

    def joined(rows):
        even, odd = rows[0:blocks], rows[blocks : 2 * blocks]
        return (
            jnp.where(low_lane, even, pltpu.roll(odd, HALF, 1)),
            jnp.where(low_lane, pltpu.roll(even, HALF, 1), odd),
        )

    def parts_of(x):
        high = x.astype(bf16)
        return high, (x - high.astype(f32)).astype(bf16)

    def dot(a, b):
        return jnp.dot(a, b, preferred_element_type=f32)

    def product_right(x, table):
        high, rest = parts_of(x)
        return dot(high, table[0]) + dot(high, table[1]) + dot(rest, table[0])

    def product_left(table, x):
        high, rest = parts_of(x)
        return dot(table[0], high) + dot(table[1], high) + dot(table[0], rest)

    def spectrum(re, im):
        cosine, sine = twiddle[0], twiddle[1]
        turned = jnp.concatenate([re * cosine - im * sine, re * sine + im * cosine], axis=1)
        return product_right(turned, inner)

    def conj_times(a, b):
        ar, ai = a[:, 0:LANES], a[:, LANES:]
        br, bi = b[:, 0:LANES], b[:, LANES:]
        return jnp.concatenate([ar * br + ai * bi, ar * bi - ai * br], axis=1)

    def unturned(x):
        y = product_right(x, outer)
        re, im = y[:, 0:LANES], y[:, LANES:]
        cosine, sine = twiddle[0], twiddle[1]
        return jnp.concatenate([re * cosine + im * sine, im * cosine - re * sine], axis=0)

    wait_all(all_taps.at[pl.ds(0, z_count - 1)], recv_sems.at[2])
    taps_wide = all_taps[...].astype(f32)

    def taps_of(f):
        return taps_wide[:, f * y_count : (f + 1) * y_count, :].reshape(blocks, LANES)

    taps_in = jnp.concatenate(
        [by_halves(taps_of(f), taps_of(f + 1)) for f in range(0, filters, 2)], axis=1
    ).astype(bf16)
    taps_first = dot(taps_tab, jnp.concatenate([taps_in, taps_in], axis=0))
    for q in range(filters // 2):
        lanes = slice(q * LANES, (q + 1) * LANES)
        spectra[q] = spectrum(taps_first[0:tall, lanes], taps_first[tall:, lanes])

    wait_all(recv1.at[pl.ds(0, seq_count - 1)], recv_sems.at[1])
    wide1[...] = recv1[...].astype(f32).reshape(blocks * 16, LANES)

    def first_stage(base):
        columns = []
        for f in range(0, filters, 2):
            rows = [
                by_halves(
                    wide1[pl.ds(base + a * filters + f, blocks, stride=16), :],
                    wide1[pl.ds(base + a * filters + f + 1, blocks, stride=16), :],
                )
                for a in range(2)
            ]
            columns.append(jnp.concatenate(rows, axis=0))
        data = jnp.concatenate(columns, axis=1).astype(bf16)
        return dot(left[...], jnp.concatenate([data, data], axis=0))

    grad_first = first_stage(0)
    value_first = first_stage(8)
    grad_back, lag_back = [], []
    for q in range(filters // 2):
        lanes = slice(q * LANES, (q + 1) * LANES)
        grad_spec = spectrum(grad_first[0:tall, lanes], grad_first[tall:, lanes])
        value_spec = spectrum(value_first[0:tall, lanes], value_first[tall:, lanes])
        grad_back.append(unturned(conj_times(spectra[q], grad_spec)))
        lag_back.append(unturned(conj_times(value_spec, grad_spec)))
    in_grad = product_left(left_back, jnp.concatenate(grad_back, axis=1)) * scale
    lag_sums = product_left(lags_tab, jnp.concatenate(lag_back, axis=1)) * scale

    for q in range(filters // 2):
        lanes = slice(q * LANES, (q + 1) * LANES)
        for a in range(2):
            for n, rows in enumerate(joined(in_grad[a * halves : (a + 1) * halves, lanes])):
                wide2[pl.ds(a * filters + 2 * q + n, blocks, stride=16), :] = rows
        for n, rows in enumerate(joined(lag_sums[:, lanes])):
            rounded = rows.astype(bf16).astype(f32)
            wide2[pl.ds(8 + 2 * q + n, blocks, stride=16), :] = rounded
            wide2[pl.ds(8 + filters + 2 * q + n, blocks, stride=16), :] = rows - rounded
    send2[...] = wide2[...].reshape(blocks, 16, LANES).astype(bf16)

    def send_back(d, carry):
        to = partner(d)
        pltpu.make_async_remote_copy(
            src_ref=send2.at[to],
            dst_ref=recv2.at[me],
            send_sem=send_sems.at[3],
            recv_sem=recv_sems.at[3],
            device_id={"seq": to},
            device_id_type=MESH,
        ).start()
        return carry

    lax.fori_loop(1, seq_count, send_back, 0)
    recv2[me] = send2[me]
    wait_all(recv2.at[pl.ds(0, seq_count - 1)], recv_sems.at[3])

    def add_lags(p, total):
        return total + recv2[p].astype(f32)

    summed = lax.fori_loop(0, seq_count, add_lags, jnp.zeros((16, LANES), f32))
    part[...] = summed[8:16]

    def send_ch(d, carry):
        pltpu.make_async_remote_copy(
            src_ref=part,
            dst_ref=parts.at[my_ch],
            send_sem=send_sems.at[4],
            recv_sem=recv_sems.at[4],
            device_id={"ch": lax.rem(my_ch + d, ch_count)},
            device_id_type=MESH,
        ).start()
        return carry

    lax.fori_loop(1, ch_count, send_ch, 0)
    parts[my_ch] = part[...]

    for c in range(vg_ref.shape[1] // LANES):
        rows = recv2[pl.ds(c * group, group)].astype(f32)[:, 0:8, :].reshape(LANES, LANES)
        vg_ref[:, pl.ds(c * LANES, LANES)] = rows.T.astype(bf16)

    wait_all(parts.at[pl.ds(0, ch_count - 1)], recv_sems.at[4])
    both = jnp.sum(parts[...], axis=0)
    fg_ref[...] = both[0:filters] + both[filters : 2 * filters]

    wait_all(row_taps.at[pl.ds(0, (y_count - 1) * 8)], send_sems.at[0])
    wait_all(send1.at[pl.ds(0, seq_count - 1)], send_sems.at[1])
    wait_all(all_taps.at[pl.ds(0, z_count - 1)], send_sems.at[2])
    wait_all(send2.at[pl.ds(0, seq_count - 1)], send_sems.at[3])
    wait_all(parts.at[pl.ds(0, ch_count - 1)], send_sems.at[4])


def local(upstream_grad, gate_act, value_act, filter_taps, half_ids):
    seq_count = lax.axis_size("seq")
    ch_count = lax.axis_size("ch")
    local_rows, channels = upstream_grad.shape
    filters = filter_taps.shape[0]
    blocks = seq_count
    halves = 2 * blocks
    tall = 2 * halves
    y_count = 1 << ((seq_count.bit_length() - 1) // 2)
    f32, bf16 = jnp.float32, jnp.bfloat16
    twiddle, pieces = tables(halves)
    width = max(tall, 2 * LANES)
    matrix = np.concatenate([np.pad(x, ((0, 0), (0, width - x.shape[1]))) for x in pieces], 0)
    constants = [jnp.asarray(twiddle), jnp.asarray(matrix)]
    vmem = pl.BlockSpec(memory_space=pltpu.VMEM)
    operands = [upstream_grad, gate_act, value_act, filter_taps, half_ids] + constants
    return pl.pallas_call(
        functools.partial(kernel, seq_count, ch_count),
        out_shape=(
            jax.ShapeDtypeStruct((local_rows, channels), bf16),
            jax.ShapeDtypeStruct((filters, LANES), f32),
        ),
        in_specs=[pl.BlockSpec(memory_space=pl.ANY)] * len(operands),
        out_specs=(vmem, vmem),
        scratch_shapes=[pltpu.VMEM(x.shape, x.dtype) for x in operands]
        + [
            pltpu.VMEM((y_count * 8, LANES), f32),
            pltpu.VMEM((filters * y_count, LANES), bf16),
            pltpu.VMEM((seq_count // y_count, filters * y_count, LANES), bf16),
            pltpu.VMEM((seq_count, 16, LANES), bf16),
            pltpu.VMEM((seq_count, 16, LANES), bf16),
            pltpu.VMEM((blocks * 16, LANES), f32),
            pltpu.VMEM((2 * tall, 2 * tall), bf16),
            pltpu.VMEM((2, 2 * halves, 2 * tall), bf16),
            pltpu.VMEM((filters // 2, tall, 2 * LANES), f32),
            pltpu.VMEM((blocks * 16, LANES), f32),
            pltpu.VMEM((seq_count, 16, LANES), bf16),
            pltpu.VMEM((seq_count, 16, LANES), bf16),
            pltpu.VMEM((8, LANES), f32),
            pltpu.VMEM((ch_count, 8, LANES), f32),
            pltpu.SemaphoreType.DMA((len(operands),)),
            pltpu.SemaphoreType.DMA((5,)),
            pltpu.SemaphoreType.DMA((5,)),
        ],
        compiler_params=pltpu.CompilerParams(
            collective_id=0, has_side_effects=True, vmem_limit_bytes=60 * 1024 * 1024
        ),
        cost_estimate=pl.CostEstimate(
            flops=40 * 2 * 256**3,
            bytes_accessed=4 * local_rows * channels * 2,
            transcendentals=0,
        ),
    )(*operands)


def solution(mesh):
    placed = (P("seq", "ch"), P("seq", "ch"), P("seq", "ch"), P(None, "seq"), P())
    return jax.shard_map(
        local,
        mesh=mesh,
        in_specs=placed,
        out_specs=(P("seq", "ch"), P(None, "seq")),
        check_vma=False,
    )
```

```python
import functools
import math

import jax
import jax.numpy as jnp
import ml_dtypes
import numpy as np
from jax import lax
from jax.experimental import pallas as pl
from jax.experimental.pallas import tpu as pltpu
from jax.sharding import PartitionSpec as P

MESH = pl.DeviceIdType.MESH
LANES = 128
HALF = 64


def two_parts(table):
    high = table.astype(ml_dtypes.bfloat16)
    rest = (table - high.astype(np.float64)).astype(ml_dtypes.bfloat16)
    return high, rest


@functools.lru_cache(maxsize=None)
def tables(halves):
    tall = 2 * halves
    points = tall * HALF
    angle = 2 * np.pi * np.outer(np.arange(tall), np.arange(halves)) / tall
    cosine, sine = np.cos(angle), -np.sin(angle)
    parts = two_parts(cosine) + two_parts(sine)
    forward = np.concatenate([np.concatenate(parts[0:2], 0), np.concatenate(parts[2:4], 0)], 1)
    back = np.concatenate([part.T for part in parts], 0)
    natural = np.concatenate([np.arange(0, halves, 2), np.arange(1, halves, 2)])
    both = np.concatenate([cosine, sine], 0)[:, natural]
    taps = np.concatenate(two_parts(both), 1)
    lags = np.concatenate(two_parts(cosine.T[natural]) + two_parts(sine.T[natural]), 0)
    turn = 2 * np.pi * np.outer(np.arange(tall), np.arange(HALF)) / points
    turn = np.tile(turn, (1, 2))
    twiddle = np.stack([np.cos(turn), -np.sin(turn)]).astype(np.float32)
    small = 2 * np.pi * np.outer(np.arange(HALF), np.arange(HALF)) / HALF
    pair = np.eye(2)
    real, imag = np.kron(pair, np.cos(small)), np.kron(pair, -np.sin(small))
    inner = two_parts(np.block([[real, imag], [-imag, real]]))
    outer = two_parts(np.block([[real, -imag], [imag, real]]))
    return twiddle, (forward, back, taps, lags) + inner + outer


def kernel(
    seq_count,
    ch_count,
    up_hbm,
    gate_hbm,
    value_hbm,
    taps_hbm,
    ids_hbm,
    twiddle_hbm,
    matrix_hbm,
    vg_ref,
    fg_ref,
    up_ref,
    gate_ref,
    value_ref,
    taps_ref,
    ids_ref,
    twiddle,
    matrix,
    row_taps,
    packed_taps,
    all_taps,
    send1,
    recv1,
    wide1,
    left,
    left_back,
    lag_send,
    lag_recv,
    send2,
    recv2,
    part,
    parts,
    load_sems,
    send_sems,
    recv_sems,
):
    f32, bf16 = jnp.float32, jnp.bfloat16
    y_count = 1 << ((seq_count.bit_length() - 1) // 2)
    z_count = seq_count // y_count
    me = lax.axis_index("seq")
    my_ch = lax.axis_index("ch")
    my_z, my_y = lax.div(me, y_count), lax.rem(me, y_count)
    blocks = seq_count
    halves = 2 * blocks
    tall = 2 * halves
    filters = taps_ref.shape[0]
    scale = 1.0 / math.sqrt(blocks * LANES) / (tall * HALF)

    pairs = (
        (up_hbm, up_ref),
        (gate_hbm, gate_ref),
        (value_hbm, value_ref),
        (taps_hbm, taps_ref),
        (ids_hbm, ids_ref),
        (twiddle_hbm, twiddle),
        (matrix_hbm, matrix),
    )
    loads = [
        pltpu.make_async_copy(src, dst, load_sems.at[i]) for i, (src, dst) in enumerate(pairs)
    ]
    for load in loads:
        load.start()

    steps = sorted(
        ((dz, dy) for dz in range(z_count) for dy in range(y_count) if dz + dy > 0),
        key=lambda step: -min(step[0], z_count - step[0]) - min(step[1], y_count - step[1]),
    )
    partners = [
        lax.rem(my_z + dz, z_count) * y_count + lax.rem(my_y + dy, y_count) for dz, dy in steps
    ]

    barrier = pltpu.get_barrier_semaphore()

    for to in partners:
        pl.semaphore_signal(barrier, inc=1, device_id={"seq": to}, device_id_type=MESH)

    for d in range(1, ch_count):
        pl.semaphore_signal(
            barrier, inc=1, device_id={"ch": lax.rem(my_ch + d, ch_count)}, device_id_type=MESH
        )

    for load in loads[0:4]:
        load.wait()
    own = taps_ref[...].astype(f32)
    row_taps[pl.ds(pl.multiple_of(my_y * 8, 8), 8), :] = jnp.concatenate([own, own], axis=0)

    group = LANES // 8
    for c in range(up_ref.shape[1] // LANES):
        cols = pl.ds(c * LANES, LANES)
        product = up_ref[:, cols].astype(f32) * gate_ref[:, cols].astype(f32)
        value = value_ref[:, cols].astype(f32)
        send1[pl.ds(c * group, group)] = jnp.concatenate(
            [product.T.reshape(group, 8, LANES), value.T.reshape(group, 8, LANES)], axis=1
        ).astype(bf16)

    pl.semaphore_wait(barrier, seq_count - 1 + ch_count - 1)

    def send_y(d, carry):
        mine = row_taps.at[pl.ds(pl.multiple_of(my_y * 8, 8), 8)]
        pltpu.make_async_remote_copy(
            src_ref=mine,
            dst_ref=mine,
            send_sem=send_sems.at[0],
            recv_sem=recv_sems.at[0],
            device_id={"seq": my_z * y_count + lax.rem(my_y + d, y_count)},
            device_id_type=MESH,
        ).start()
        return carry

    lax.fori_loop(1, y_count, send_y, 0)

    for to in partners:
        pltpu.make_async_remote_copy(
            src_ref=send1.at[to],
            dst_ref=recv1.at[me],
            send_sem=send_sems.at[1],
            recv_sem=recv_sems.at[1],
            device_id={"seq": to},
            device_id_type=MESH,
        ).start()
    recv1[me] = send1[me]

    def wait_all(ref, sem):
        pltpu.make_async_copy(ref, ref, sem).wait()

    wait_all(row_taps.at[pl.ds(0, (y_count - 1) * 8)], recv_sems.at[0])

    packed_taps[...] = jnp.concatenate(
        [row_taps[pl.ds(f, y_count, stride=8), :] for f in range(filters)], axis=0
    ).astype(bf16)

    def send_z(d, carry):
        pltpu.make_async_remote_copy(
            src_ref=packed_taps,
            dst_ref=all_taps.at[my_z],
            send_sem=send_sems.at[2],
            recv_sem=recv_sems.at[2],
            device_id={"seq": lax.rem(my_z + d, z_count) * y_count + my_y},
            device_id_type=MESH,
        ).start()
        return carry

    lax.fori_loop(1, z_count, send_z, 0)
    all_taps[my_z] = packed_taps[...]

    for load in loads[4:]:
        load.wait()
    slot = lax.broadcasted_iota(jnp.int32, (halves, halves), 0)
    column = lax.broadcasted_iota(jnp.int32, (halves, halves), 1)
    split = (2 * lax.rem(column, blocks) + lax.div(column, blocks) == slot).astype(bf16)
    ids = ids_ref[...].reshape(1, halves).astype(f32).astype(bf16)
    split_ids = jnp.dot(ids, split, preferred_element_type=f32).astype(jnp.int32)
    place = jnp.where(slot == split_ids, 1.0, 0.0)
    chooser, chooser_rows = place.astype(bf16), place.T.astype(bf16)

    def table(start, rows, first=0, columns=tall):
        return matrix[start : start + rows, first : first + columns]

    for n in range(2):
        cosine = jnp.dot(table(n * tall, tall, 0, halves), chooser, preferred_element_type=f32)
        sine = jnp.dot(table(n * tall, tall, halves, halves), chooser, preferred_element_type=f32)
        left[0:tall, n * tall : (n + 1) * tall] = jnp.concatenate([cosine, -sine], axis=1).astype(bf16)
        left[tall : 2 * tall, n * tall : (n + 1) * tall] = jnp.concatenate([sine, cosine], axis=1).astype(
            bf16
        )
        start = 2 * tall + n * halves
        cosine = jnp.dot(chooser_rows, table(start, halves), preferred_element_type=f32)
        sine = jnp.dot(chooser_rows, table(start + tall, halves), preferred_element_type=f32)
        left_back[n, 0:halves, :] = jnp.concatenate([cosine, sine], axis=1).astype(bf16)
        left_back[n, halves : 2 * halves, :] = jnp.concatenate([-sine, cosine], axis=1).astype(bf16)

    taps_tab = table(4 * tall, 2 * tall)
    start = 6 * tall
    lags_tab = [
        jnp.concatenate(
            [table(start + n * halves, halves), table(start + tall + n * halves, halves)], axis=1
        )
        for n in range(2)
    ]
    inner_rows, outer_rows = 8 * tall, 8 * tall + 4 * LANES
    inner = [table(inner_rows + n * 2 * LANES, 2 * LANES, 0, 2 * LANES) for n in range(2)]
    outer = [table(outer_rows + n * 2 * LANES, 2 * LANES, 0, 2 * LANES) for n in range(2)]

    low_lane = lax.broadcasted_iota(jnp.int32, (blocks, LANES), 1) < HALF

    def by_halves(rows0, rows1):
        return jnp.concatenate(
            [
                jnp.where(low_lane, rows0, pltpu.roll(rows1, HALF, 1)),
                jnp.where(low_lane, pltpu.roll(rows0, HALF, 1), rows1),
            ],
            axis=0,
        )

    def joined(rows):
        even, odd = rows[0:blocks], rows[blocks : 2 * blocks]
        return (
            jnp.where(low_lane, even, pltpu.roll(odd, HALF, 1)),
            jnp.where(low_lane, pltpu.roll(even, HALF, 1), odd),
        )

    def parts_of(x):
        high = x.astype(bf16)
        return high, (x - high.astype(f32)).astype(bf16)

    def dot(a, b):
        return jnp.dot(a, b, preferred_element_type=f32)

    def product_right(x, table):
        high, rest = parts_of(x)
        return dot(high, table[0]) + dot(high, table[1]) + dot(rest, table[0])

    def product_left(table, x):
        high, rest = parts_of(x)
        return dot(table[0], high) + dot(table[1], high) + dot(table[0], rest)

    def spectrum(re, im):
        cosine, sine = twiddle[0], twiddle[1]
        turned = jnp.concatenate([re * cosine - im * sine, re * sine + im * cosine], axis=1)
        return product_right(turned, inner)

    def conj_times(a, b):
        ar, ai = a[:, 0:LANES], a[:, LANES:]
        br, bi = b[:, 0:LANES], b[:, LANES:]
        return jnp.concatenate([ar * br + ai * bi, ar * bi - ai * br], axis=1)

    def unturned(x):
        y = product_right(x, outer)
        re, im = y[:, 0:LANES], y[:, LANES:]
        cosine, sine = twiddle[0], twiddle[1]
        return jnp.concatenate([re * cosine + im * sine, im * cosine - re * sine], axis=0)

    wait_all(recv1.at[pl.ds(0, seq_count - 1)], recv_sems.at[1])
    wide1[...] = recv1[...].astype(f32).reshape(blocks * 16, LANES)

    def first_stage(base):
        columns = []
        for f in range(0, filters, 2):
            rows = [
                by_halves(
                    wide1[pl.ds(base + a * filters + f, blocks, stride=16), :],
                    wide1[pl.ds(base + a * filters + f + 1, blocks, stride=16), :],
                )
                for a in range(2)
            ]
            columns.append(jnp.concatenate(rows, axis=0))
        data = jnp.concatenate(columns, axis=1).astype(bf16)
        return dot(left[...], jnp.concatenate([data, data], axis=0))

    grad_first = first_stage(0)
    value_first = first_stage(8)
    grad_spectra, lag_back = [], []
    for q in range(filters // 2):
        lanes = slice(q * LANES, (q + 1) * LANES)
        grad_spec = spectrum(grad_first[0:tall, lanes], grad_first[tall:, lanes])
        value_spec = spectrum(value_first[0:tall, lanes], value_first[tall:, lanes])
        grad_spectra.append(grad_spec)
        lag_back.append(unturned(conj_times(value_spec, grad_spec)))
    lag_sums = product_left(lags_tab, jnp.concatenate(lag_back, axis=1)) * scale

    for q in range(filters // 2):
        for n, rows in enumerate(joined(lag_sums[:, q * LANES : (q + 1) * LANES])):
            lag_send[:, 2 * q + n, :] = rows
    for to in partners:
        pltpu.make_async_remote_copy(
            src_ref=lag_send.at[to],
            dst_ref=lag_recv.at[me],
            send_sem=send_sems.at[5],
            recv_sem=recv_sems.at[5],
            device_id={"seq": to},
            device_id_type=MESH,
        ).start()
    lag_recv[me] = lag_send[me]

    wait_all(all_taps.at[pl.ds(0, z_count - 1)], recv_sems.at[2])
    taps_wide = all_taps[...].astype(f32)

    def taps_of(f):
        return taps_wide[:, f * y_count : (f + 1) * y_count, :].reshape(blocks, LANES)

    taps_in = jnp.concatenate(
        [by_halves(taps_of(f), taps_of(f + 1)) for f in range(0, filters, 2)], axis=1
    ).astype(bf16)
    taps_first = dot(taps_tab, jnp.concatenate([taps_in, taps_in], axis=0))
    grad_back = []
    for q in range(filters // 2):
        lanes = slice(q * LANES, (q + 1) * LANES)
        taps_spec = spectrum(taps_first[0:tall, lanes], taps_first[tall:, lanes])
        grad_back.append(unturned(conj_times(taps_spec, grad_spectra[q])))

    in_grad = product_left(left_back, jnp.concatenate(grad_back, axis=1)) * scale
    for q in range(filters // 2):
        lanes = slice(q * LANES, (q + 1) * LANES)
        for a in range(2):
            for n, rows in enumerate(joined(in_grad[a * halves : (a + 1) * halves, lanes])):
                send2[:, a * filters + 2 * q + n, :] = rows
    for to in partners:
        pltpu.make_async_remote_copy(
            src_ref=send2.at[to],
            dst_ref=recv2.at[me],
            send_sem=send_sems.at[3],
            recv_sem=recv_sems.at[3],
            device_id={"seq": to},
            device_id_type=MESH,
        ).start()
    recv2[me] = send2[me]

    wait_all(lag_recv.at[pl.ds(0, seq_count - 1)], recv_sems.at[5])
    part[...] = jnp.sum(lag_recv[...], axis=0)
    for d in range(1, ch_count):
        pltpu.make_async_remote_copy(
            src_ref=part,
            dst_ref=parts.at[my_ch],
            send_sem=send_sems.at[4],
            recv_sem=recv_sems.at[4],
            device_id={"ch": lax.rem(my_ch + d, ch_count)},
            device_id_type=MESH,
        ).start()
    parts[my_ch] = part[...]

    wait_all(recv2.at[pl.ds(0, seq_count - 1)], recv_sems.at[3])
    for c in range(vg_ref.shape[1] // LANES):
        rows = recv2[pl.ds(c * group, group)].reshape(LANES, LANES)
        vg_ref[:, pl.ds(c * LANES, LANES)] = rows.T.astype(bf16)

    wait_all(parts.at[pl.ds(0, ch_count - 1)], recv_sems.at[4])
    fg_ref[...] = jnp.sum(parts[...], axis=0)

    wait_all(row_taps.at[pl.ds(0, (y_count - 1) * 8)], send_sems.at[0])
    wait_all(send1.at[pl.ds(0, seq_count - 1)], send_sems.at[1])
    wait_all(all_taps.at[pl.ds(0, z_count - 1)], send_sems.at[2])
    wait_all(lag_send.at[pl.ds(0, seq_count - 1)], send_sems.at[5])
    wait_all(send2.at[pl.ds(0, seq_count - 1)], send_sems.at[3])
    wait_all(parts.at[pl.ds(0, ch_count - 1)], send_sems.at[4])


def local(upstream_grad, gate_act, value_act, filter_taps, half_ids):
    seq_count = lax.axis_size("seq")
    ch_count = lax.axis_size("ch")
    local_rows, channels = upstream_grad.shape
    filters = filter_taps.shape[0]
    blocks = seq_count
    halves = 2 * blocks
    tall = 2 * halves
    y_count = 1 << ((seq_count.bit_length() - 1) // 2)
    f32, bf16 = jnp.float32, jnp.bfloat16
    twiddle, pieces = tables(halves)
    width = max(tall, 2 * LANES)
    matrix = np.concatenate([np.pad(x, ((0, 0), (0, width - x.shape[1]))) for x in pieces], 0)
    constants = [jnp.asarray(twiddle), jnp.asarray(matrix)]
    vmem = pl.BlockSpec(memory_space=pltpu.VMEM)
    operands = [upstream_grad, gate_act, value_act, filter_taps, half_ids] + constants
    return pl.pallas_call(
        functools.partial(kernel, seq_count, ch_count),
        out_shape=(
            pltpu.VMEM((local_rows, channels), bf16),
            pltpu.VMEM((filters, LANES), f32),
        ),
        in_specs=[pl.BlockSpec(memory_space=pl.ANY)] * len(operands),
        out_specs=(vmem, vmem),
        scratch_shapes=[pltpu.VMEM(x.shape, x.dtype) for x in operands]
        + [
            pltpu.VMEM((y_count * 8, LANES), f32),
            pltpu.VMEM((filters * y_count, LANES), bf16),
            pltpu.VMEM((seq_count // y_count, filters * y_count, LANES), bf16),
            pltpu.VMEM((seq_count, 16, LANES), bf16),
            pltpu.VMEM((seq_count, 16, LANES), bf16),
            pltpu.VMEM((blocks * 16, LANES), f32),
            pltpu.VMEM((2 * tall, 2 * tall), bf16),
            pltpu.VMEM((2, 2 * halves, 2 * tall), bf16),
            pltpu.VMEM((seq_count, filters, LANES), f32),
            pltpu.VMEM((seq_count, filters, LANES), f32),
            pltpu.VMEM((seq_count, 8, LANES), f32),
            pltpu.VMEM((seq_count, 8, LANES), f32),
            pltpu.VMEM((filters, LANES), f32),
            pltpu.VMEM((ch_count, filters, LANES), f32),
            pltpu.SemaphoreType.DMA((len(operands),)),
            pltpu.SemaphoreType.DMA((6,)),
            pltpu.SemaphoreType.DMA((6,)),
        ],
        compiler_params=pltpu.CompilerParams(
            collective_id=0, has_side_effects=True, vmem_limit_bytes=60 * 1024 * 1024
        ),
        cost_estimate=pl.CostEstimate(
            flops=40 * 2 * 256**3,
            bytes_accessed=4 * local_rows * channels * 2,
            transcendentals=0,
        ),
    )(*operands)


def solution(mesh):
    placed = (P("seq", "ch"), P("seq", "ch"), P("seq", "ch"), P(None, "seq"), P())
    return jax.shard_map(
        local,
        mesh=mesh,
        in_specs=placed,
        out_specs=(P("seq", "ch"), P(None, "seq")),
        check_vma=False,
    )
```

```python
import functools
import math

import jax
import jax.numpy as jnp
import ml_dtypes
import numpy as np
from jax import lax
from jax.experimental import pallas as pl
from jax.experimental.pallas import tpu as pltpu
from jax.sharding import PartitionSpec as P

MESH = pl.DeviceIdType.MESH
LANES = 128
HALF = 64


def two_parts(table):
    high = table.astype(ml_dtypes.bfloat16)
    rest = (table - high.astype(np.float64)).astype(ml_dtypes.bfloat16)
    return high, rest


@functools.lru_cache(maxsize=None)
def tables(halves):
    tall = 2 * halves
    points = tall * HALF
    angle = 2 * np.pi * np.outer(np.arange(halves), np.arange(halves)) / tall
    cosine, sine = np.cos(angle), -np.sin(angle)
    sine[0] = np.cos(np.pi * np.arange(halves))
    both = np.concatenate([cosine, sine], 0)
    natural = np.concatenate([np.arange(0, halves, 2), np.arange(1, halves, 2)])
    forward = np.concatenate(two_parts(both), 1)
    back = np.concatenate(two_parts(both.T), 0)
    taps = np.concatenate(two_parts(both[:, natural]), 1)
    lags = np.concatenate(two_parts(both.T[natural]), 0)
    order = np.concatenate([np.arange(halves + 1), np.arange(tall - 1, halves, -1)])
    turn = 2 * np.pi * np.outer(order, np.arange(HALF)) / points
    turn = np.tile(turn, (1, 2))
    twiddle = np.stack([np.cos(turn), -np.sin(turn)]).astype(np.float32)
    small = 2 * np.pi * np.outer(np.arange(HALF), np.arange(HALF)) / HALF
    pair = np.eye(2)
    real, imag = np.kron(pair, np.cos(small)), np.kron(pair, -np.sin(small))
    inner = two_parts(np.block([[real, imag], [-imag, real]]))
    outer = two_parts(np.block([[real, -imag], [imag, real]]))
    return twiddle, (forward, back, taps, lags) + inner + outer


def kernel(
    seq_count,
    ch_count,
    up_hbm,
    gate_hbm,
    value_hbm,
    taps_hbm,
    ids_hbm,
    twiddle_hbm,
    matrix_hbm,
    vg_ref,
    fg_ref,
    up_ref,
    gate_ref,
    value_ref,
    taps_ref,
    ids_ref,
    twiddle,
    matrix,
    row_taps,
    packed_taps,
    all_taps,
    send1,
    recv1,
    wide1,
    left,
    left_back,
    lag_send,
    lag_recv,
    send2,
    recv2,
    part,
    parts,
    load_sems,
    send_sems,
    recv_sems,
):
    f32, bf16 = jnp.float32, jnp.bfloat16
    y_count = 1 << ((seq_count.bit_length() - 1) // 2)
    z_count = seq_count // y_count
    me = lax.axis_index("seq")
    my_ch = lax.axis_index("ch")
    my_z, my_y = lax.div(me, y_count), lax.rem(me, y_count)
    blocks = seq_count
    halves = 2 * blocks
    tall = 2 * halves
    filters = taps_ref.shape[0]
    scale = 1.0 / math.sqrt(blocks * LANES) / (tall * HALF)

    pairs = (
        (up_hbm, up_ref),
        (gate_hbm, gate_ref),
        (value_hbm, value_ref),
        (taps_hbm, taps_ref),
        (ids_hbm, ids_ref),
        (twiddle_hbm, twiddle),
        (matrix_hbm, matrix),
    )
    loads = [
        pltpu.make_async_copy(src, dst, load_sems.at[i]) for i, (src, dst) in enumerate(pairs)
    ]
    for load in loads:
        load.start()

    steps = sorted(
        ((dz, dy) for dz in range(z_count) for dy in range(y_count) if dz + dy > 0),
        key=lambda step: -min(step[0], z_count - step[0]) - min(step[1], y_count - step[1]),
    )
    partners = [
        lax.rem(my_z + dz, z_count) * y_count + lax.rem(my_y + dy, y_count) for dz, dy in steps
    ]

    barrier = pltpu.get_barrier_semaphore()

    for to in partners:
        pl.semaphore_signal(barrier, inc=1, device_id={"seq": to}, device_id_type=MESH)

    for d in range(1, ch_count):
        pl.semaphore_signal(
            barrier, inc=1, device_id={"ch": lax.rem(my_ch + d, ch_count)}, device_id_type=MESH
        )

    for load in loads[0:4]:
        load.wait()
    own = taps_ref[...].astype(f32)
    row_taps[pl.ds(pl.multiple_of(my_y * 8, 8), 8), :] = jnp.concatenate([own, own], axis=0)

    group = LANES // 8
    for c in range(up_ref.shape[1] // LANES):
        cols = pl.ds(c * LANES, LANES)
        product = up_ref[:, cols].astype(f32) * gate_ref[:, cols].astype(f32)
        value = value_ref[:, cols].astype(f32)
        send1[pl.ds(c * group, group)] = jnp.concatenate(
            [product.T.reshape(group, 8, LANES), value.T.reshape(group, 8, LANES)], axis=1
        ).astype(bf16)

    pl.semaphore_wait(barrier, seq_count - 1 + ch_count - 1)

    def send_y(d, carry):
        mine = row_taps.at[pl.ds(pl.multiple_of(my_y * 8, 8), 8)]
        pltpu.make_async_remote_copy(
            src_ref=mine,
            dst_ref=mine,
            send_sem=send_sems.at[0],
            recv_sem=recv_sems.at[0],
            device_id={"seq": my_z * y_count + lax.rem(my_y + d, y_count)},
            device_id_type=MESH,
        ).start()
        return carry

    lax.fori_loop(1, y_count, send_y, 0)

    for to in partners:
        pltpu.make_async_remote_copy(
            src_ref=send1.at[to],
            dst_ref=recv1.at[me],
            send_sem=send_sems.at[1],
            recv_sem=recv_sems.at[1],
            device_id={"seq": to},
            device_id_type=MESH,
        ).start()
    recv1[me] = send1[me]

    def wait_all(ref, sem):
        pltpu.make_async_copy(ref, ref, sem).wait()

    wait_all(row_taps.at[pl.ds(0, (y_count - 1) * 8)], recv_sems.at[0])

    packed_taps[...] = jnp.concatenate(
        [row_taps[pl.ds(f, y_count, stride=8), :] for f in range(filters)], axis=0
    ).astype(bf16)

    def send_z(d, carry):
        pltpu.make_async_remote_copy(
            src_ref=packed_taps,
            dst_ref=all_taps.at[my_z],
            send_sem=send_sems.at[2],
            recv_sem=recv_sems.at[2],
            device_id={"seq": lax.rem(my_z + d, z_count) * y_count + my_y},
            device_id_type=MESH,
        ).start()
        return carry

    lax.fori_loop(1, z_count, send_z, 0)
    all_taps[my_z] = packed_taps[...]

    for load in loads[4:]:
        load.wait()
    slot = lax.broadcasted_iota(jnp.int32, (halves, halves), 0)
    column = lax.broadcasted_iota(jnp.int32, (halves, halves), 1)
    split = (2 * lax.rem(column, blocks) + lax.div(column, blocks) == slot).astype(bf16)
    ids = ids_ref[...].reshape(1, halves).astype(f32).astype(bf16)
    split_ids = jnp.dot(ids, split, preferred_element_type=f32).astype(jnp.int32)
    place = jnp.where(slot == split_ids, 1.0, 0.0)
    chooser, chooser_rows = place.astype(bf16), place.T.astype(bf16)

    def table(start, rows, first=0, columns=tall):
        return matrix[start : start + rows, first : first + columns]

    for n in range(2):
        left[:, n * halves : (n + 1) * halves] = jnp.dot(
            table(0, tall, n * halves, halves), chooser, preferred_element_type=f32
        ).astype(bf16)
        left_back[n] = jnp.dot(
            chooser_rows, table(tall + n * halves, halves), preferred_element_type=f32
        ).astype(bf16)

    taps_tab = table(2 * tall, tall)
    lags_tab = [table(3 * tall + n * halves, halves) for n in range(2)]
    inner_rows, outer_rows = 4 * tall, 4 * tall + 4 * LANES
    inner = [table(inner_rows + n * 2 * LANES, 2 * LANES, 0, 2 * LANES) for n in range(2)]
    outer = [table(outer_rows + n * 2 * LANES, 2 * LANES, 0, 2 * LANES) for n in range(2)]

    low_lane = lax.broadcasted_iota(jnp.int32, (blocks, LANES), 1) < HALF
    top_row = lax.broadcasted_iota(jnp.int32, (halves, LANES), 0) == 0

    def by_halves(rows0, rows1):
        return jnp.concatenate(
            [
                jnp.where(low_lane, rows0, pltpu.roll(rows1, HALF, 1)),
                jnp.where(low_lane, pltpu.roll(rows0, HALF, 1), rows1),
            ],
            axis=0,
        )

    def joined(rows):
        even, odd = rows[0:blocks], rows[blocks : 2 * blocks]
        return (
            jnp.where(low_lane, even, pltpu.roll(odd, HALF, 1)),
            jnp.where(low_lane, pltpu.roll(even, HALF, 1), odd),
        )

    def parts_of(x):
        high = x.astype(bf16)
        return high, (x - high.astype(f32)).astype(bf16)

    def dot(a, b):
        return jnp.dot(a, b, preferred_element_type=f32)

    def product_right(x, table):
        high, rest = parts_of(x)
        return dot(high, table[0]) + dot(high, table[1]) + dot(rest, table[0])

    def product_left(table, x):
        high, rest = parts_of(x)
        return dot(table[0], high) + dot(table[1], high) + dot(table[0], rest)

    def spectrum(re, im):
        cosine, sine = twiddle[0], twiddle[1]
        turned = jnp.concatenate([re * cosine - im * sine, re * sine + im * cosine], axis=1)
        return product_right(turned, inner)

    def conj_times(a, b):
        ar, ai = a[:, 0:LANES], a[:, LANES:]
        br, bi = b[:, 0:LANES], b[:, LANES:]
        return jnp.concatenate([ar * br + ai * bi, ar * bi - ai * br], axis=1)

    def unturned(x):
        y = product_right(x, outer)
        re, im = y[:, 0:LANES], y[:, LANES:]
        cosine, sine = twiddle[0], twiddle[1]
        re, im = re * cosine + im * sine, im * cosine - re * sine
        re, re_pair, im, im_pair = re[0:halves], re[halves:], im[0:halves], im[halves:]
        real = [jnp.where(top_row, re, re + re_pair), jnp.where(top_row, re_pair, im - im_pair)]
        imag = [jnp.where(top_row, im, im + im_pair), jnp.where(top_row, im_pair, re_pair - re)]
        return jnp.concatenate(real, axis=0), jnp.concatenate(imag, axis=0)

    def unfolded(of_real, of_imag=None):
        cos_re, sin_re = of_real[0:halves], of_real[halves:]
        sin_low = jnp.where(top_row, 0.0, sin_re)
        if of_imag is None:
            re = [cos_re, jnp.where(top_row, sin_re, cos_re)]
            im = [sin_low, -sin_low]
        else:
            cos_im, sin_im = of_imag[0:halves], of_imag[halves:]
            re = [
                cos_re - jnp.where(top_row, 0.0, sin_im),
                jnp.where(top_row, sin_re, cos_re + sin_im),
            ]
            im = [cos_im + sin_low, jnp.where(top_row, sin_im, cos_im - sin_re)]
        return jnp.concatenate(re, axis=0), jnp.concatenate(im, axis=0)

    wait_all(recv1.at[pl.ds(0, seq_count - 1)], recv_sems.at[1])
    wide1[...] = recv1[...].astype(f32).reshape(blocks * 16, LANES)

    def first_stage(base):
        data = jnp.concatenate(
            [
                by_halves(
                    wide1[pl.ds(base + a * filters + f, blocks, stride=16), :],
                    wide1[pl.ds(base + a * filters + f + 1, blocks, stride=16), :],
                )
                for a in range(2)
                for f in range(0, filters, 2)
            ],
            axis=1,
        ).astype(bf16)
        return dot(left[...], jnp.concatenate([data, data], axis=0))

    grad_first = first_stage(0)
    value_first = first_stage(8)
    pairs_of_filters = filters // 2
    grad_spectra, lag_back = [], []
    for q in range(pairs_of_filters):
        real = slice(q * LANES, (q + 1) * LANES)
        imag = slice((pairs_of_filters + q) * LANES, (pairs_of_filters + q + 1) * LANES)
        grad_spec = spectrum(*unfolded(grad_first[:, real], grad_first[:, imag]))
        value_spec = spectrum(*unfolded(value_first[:, real], value_first[:, imag]))
        grad_spectra.append(grad_spec)
        lag_back.append(unturned(conj_times(value_spec, grad_spec))[0])
    lag_sums = product_left(lags_tab, jnp.concatenate(lag_back, axis=1)) * scale

    for q in range(filters // 2):
        for n, rows in enumerate(joined(lag_sums[:, q * LANES : (q + 1) * LANES])):
            lag_send[:, 2 * q + n, :] = rows
    for to in partners:
        pltpu.make_async_remote_copy(
            src_ref=lag_send.at[to],
            dst_ref=lag_recv.at[me],
            send_sem=send_sems.at[5],
            recv_sem=recv_sems.at[5],
            device_id={"seq": to},
            device_id_type=MESH,
        ).start()
    lag_recv[me] = lag_send[me]

    wait_all(all_taps.at[pl.ds(0, z_count - 1)], recv_sems.at[2])
    taps_wide = all_taps[...].astype(f32)

    def taps_of(f):
        return taps_wide[:, f * y_count : (f + 1) * y_count, :].reshape(blocks, LANES)

    taps_in = jnp.concatenate(
        [by_halves(taps_of(f), taps_of(f + 1)) for f in range(0, filters, 2)], axis=1
    ).astype(bf16)
    taps_first = dot(taps_tab, jnp.concatenate([taps_in, taps_in], axis=0))
    grad_back = []
    for q in range(filters // 2):
        lanes = slice(q * LANES, (q + 1) * LANES)
        taps_spec = spectrum(*unfolded(taps_first[:, lanes]))
        grad_back.append(unturned(conj_times(taps_spec, grad_spectra[q])))

    folded = [grad_back[q][a] for a in range(2) for q in range(pairs_of_filters)]
    in_grad = product_left(left_back, jnp.concatenate(folded, axis=1)) * scale
    for a in range(2):
        for q in range(pairs_of_filters):
            start = (a * pairs_of_filters + q) * LANES
            for n, rows in enumerate(joined(in_grad[:, start : start + LANES])):
                send2[:, a * filters + 2 * q + n, :] = rows
    for to in partners:
        pltpu.make_async_remote_copy(
            src_ref=send2.at[to],
            dst_ref=recv2.at[me],
            send_sem=send_sems.at[3],
            recv_sem=recv_sems.at[3],
            device_id={"seq": to},
            device_id_type=MESH,
        ).start()
    recv2[me] = send2[me]

    wait_all(lag_recv.at[pl.ds(0, seq_count - 1)], recv_sems.at[5])
    part[...] = jnp.sum(lag_recv[...], axis=0)
    for d in range(1, ch_count):
        pltpu.make_async_remote_copy(
            src_ref=part,
            dst_ref=parts.at[my_ch],
            send_sem=send_sems.at[4],
            recv_sem=recv_sems.at[4],
            device_id={"ch": lax.rem(my_ch + d, ch_count)},
            device_id_type=MESH,
        ).start()
    parts[my_ch] = part[...]

    wait_all(recv2.at[pl.ds(0, seq_count - 1)], recv_sems.at[3])
    for c in range(vg_ref.shape[1] // LANES):
        rows = recv2[pl.ds(c * group, group)].reshape(LANES, LANES)
        vg_ref[:, pl.ds(c * LANES, LANES)] = rows.T.astype(bf16)

    wait_all(parts.at[pl.ds(0, ch_count - 1)], recv_sems.at[4])
    fg_ref[...] = jnp.sum(parts[...], axis=0)

    wait_all(row_taps.at[pl.ds(0, (y_count - 1) * 8)], send_sems.at[0])
    wait_all(send1.at[pl.ds(0, seq_count - 1)], send_sems.at[1])
    wait_all(all_taps.at[pl.ds(0, z_count - 1)], send_sems.at[2])
    wait_all(lag_send.at[pl.ds(0, seq_count - 1)], send_sems.at[5])
    wait_all(send2.at[pl.ds(0, seq_count - 1)], send_sems.at[3])
    wait_all(parts.at[pl.ds(0, ch_count - 1)], send_sems.at[4])


def write_out(vg_ref, fg_ref, vg_out, fg_out):
    vg_out[...] = vg_ref[...]
    fg_out[...] = fg_ref[...]


def local(upstream_grad, gate_act, value_act, filter_taps, half_ids):
    seq_count = lax.axis_size("seq")
    ch_count = lax.axis_size("ch")
    local_rows, channels = upstream_grad.shape
    filters = filter_taps.shape[0]
    blocks = seq_count
    halves = 2 * blocks
    tall = 2 * halves
    y_count = 1 << ((seq_count.bit_length() - 1) // 2)
    f32, bf16 = jnp.float32, jnp.bfloat16
    twiddle, pieces = tables(halves)
    width = max(tall, 2 * LANES)
    matrix = np.concatenate([np.pad(x, ((0, 0), (0, width - x.shape[1]))) for x in pieces], 0)
    constants = [jnp.asarray(twiddle), jnp.asarray(matrix)]
    vmem = pl.BlockSpec(memory_space=pltpu.VMEM)
    operands = [upstream_grad, gate_act, value_act, filter_taps, half_ids] + constants
    results = pl.pallas_call(
        functools.partial(kernel, seq_count, ch_count),
        out_shape=(
            pltpu.VMEM((local_rows, channels), bf16),
            pltpu.VMEM((filters, LANES), f32),
        ),
        in_specs=[pl.BlockSpec(memory_space=pl.ANY)] * len(operands),
        out_specs=(vmem, vmem),
        scratch_shapes=[pltpu.VMEM(x.shape, x.dtype) for x in operands]
        + [
            pltpu.VMEM((y_count * 8, LANES), f32),
            pltpu.VMEM((filters * y_count, LANES), bf16),
            pltpu.VMEM((seq_count // y_count, filters * y_count, LANES), bf16),
            pltpu.VMEM((seq_count, 16, LANES), bf16),
            pltpu.VMEM((seq_count, 16, LANES), bf16),
            pltpu.VMEM((blocks * 16, LANES), f32),
            pltpu.VMEM((tall, tall), bf16),
            pltpu.VMEM((2, halves, tall), bf16),
            pltpu.VMEM((seq_count, filters, LANES), f32),
            pltpu.VMEM((seq_count, filters, LANES), f32),
            pltpu.VMEM((seq_count, 8, LANES), f32),
            pltpu.VMEM((seq_count, 8, LANES), f32),
            pltpu.VMEM((filters, LANES), f32),
            pltpu.VMEM((ch_count, filters, LANES), f32),
            pltpu.SemaphoreType.DMA((len(operands),)),
            pltpu.SemaphoreType.DMA((6,)),
            pltpu.SemaphoreType.DMA((6,)),
        ],
        compiler_params=pltpu.CompilerParams(
            collective_id=0, has_side_effects=True, vmem_limit_bytes=60 * 1024 * 1024
        ),
        cost_estimate=pl.CostEstimate(
            flops=40 * 2 * 256**3,
            bytes_accessed=4 * local_rows * channels * 2,
            transcendentals=0,
        ),
    )(*operands)
    return pl.pallas_call(
        write_out,
        out_shape=(
            jax.ShapeDtypeStruct((local_rows, channels), bf16),
            jax.ShapeDtypeStruct((filters, LANES), f32),
        ),
        in_specs=[vmem, vmem],
        out_specs=(vmem, vmem),
        compiler_params=pltpu.CompilerParams(vmem_limit_bytes=1024 * 1024),
    )(*results)


def solution(mesh):
    placed = (P("seq", "ch"), P("seq", "ch"), P("seq", "ch"), P(None, "seq"), P())
    return jax.shard_map(
        local,
        mesh=mesh,
        in_specs=placed,
        out_specs=(P("seq", "ch"), P(None, "seq")),
        check_vma=False,
    )
```

```python
import functools
import math

import jax
import jax.numpy as jnp
import ml_dtypes
import numpy as np
from jax import lax
from jax.experimental import pallas as pl
from jax.experimental.pallas import tpu as pltpu
from jax.sharding import PartitionSpec as P

MESH = pl.DeviceIdType.MESH
LANES = 128
HALF = 64


def two_parts(table):
    high = table.astype(ml_dtypes.bfloat16)
    rest = (table - high.astype(np.float64)).astype(ml_dtypes.bfloat16)
    return high, rest


@functools.lru_cache(maxsize=None)
def tables(halves):
    tall = 2 * halves
    points = tall * HALF
    angle = 2 * np.pi * np.outer(np.arange(halves), np.arange(halves)) / tall
    cosine, sine = np.cos(angle), -np.sin(angle)
    sine[0] = np.cos(np.pi * np.arange(halves))
    both = np.concatenate([cosine, sine], 0)
    natural = np.concatenate([np.arange(0, halves, 2), np.arange(1, halves, 2)])
    forward = np.concatenate(two_parts(both), 1)
    back = np.concatenate(two_parts(both.T), 0)
    taps = np.concatenate(two_parts(both[:, natural]), 1)
    lags = np.concatenate(two_parts(both.T[natural]), 0)
    order = np.concatenate([np.arange(halves + 1), np.arange(tall - 1, halves, -1)])
    turn = 2 * np.pi * np.outer(order, np.arange(HALF)) / points
    turn = np.tile(turn, (1, 2))
    twiddle = np.stack([np.cos(turn), -np.sin(turn)]).astype(np.float32)
    small = 2 * np.pi * np.outer(np.arange(HALF), np.arange(HALF)) / HALF
    pair = np.eye(2)
    real, imag = np.kron(pair, np.cos(small)), np.kron(pair, -np.sin(small))
    inner = two_parts(np.block([[real, imag], [-imag, real]]))
    outer = two_parts(np.block([[real, -imag], [imag, real]]))
    return twiddle, (forward, back, taps, lags) + inner + outer


def kernel(
    seq_count,
    ch_count,
    up_hbm,
    gate_hbm,
    value_hbm,
    taps_hbm,
    ids_hbm,
    twiddle_hbm,
    matrix_hbm,
    vg_ref,
    fg_ref,
    up_ref,
    gate_ref,
    value_ref,
    taps_ref,
    ids_ref,
    twiddle,
    matrix,
    row_taps,
    packed_taps,
    all_taps,
    send1,
    recv1,
    wide1,
    left,
    left_back,
    lag_send,
    lag_recv,
    send2,
    recv2,
    part,
    parts,
    load_sems,
    send_sems,
    recv_sems,
):
    f32, bf16 = jnp.float32, jnp.bfloat16
    y_count = 1 << ((seq_count.bit_length() - 1) // 2)
    z_count = seq_count // y_count
    me = lax.axis_index("seq")
    my_ch = lax.axis_index("ch")
    my_z, my_y = lax.div(me, y_count), lax.rem(me, y_count)
    blocks = seq_count
    halves = 2 * blocks
    tall = 2 * halves
    filters = taps_ref.shape[0]
    scale = 1.0 / math.sqrt(blocks * LANES) / (tall * HALF)

    pairs = (
        (up_hbm, up_ref),
        (gate_hbm, gate_ref),
        (value_hbm, value_ref),
        (taps_hbm, taps_ref),
        (ids_hbm, ids_ref),
        (twiddle_hbm, twiddle),
        (matrix_hbm, matrix),
    )
    loads = [
        pltpu.make_async_copy(src, dst, load_sems.at[i]) for i, (src, dst) in enumerate(pairs)
    ]
    for load in loads:
        load.start()

    steps = sorted(
        ((dz, dy) for dz in range(z_count) for dy in range(y_count) if dz + dy > 0),
        key=lambda step: -min(step[0], z_count - step[0]) - min(step[1], y_count - step[1]),
    )
    partners = [
        lax.rem(my_z + dz, z_count) * y_count + lax.rem(my_y + dy, y_count) for dz, dy in steps
    ]

    barrier = pltpu.get_barrier_semaphore()

    for to in partners:
        pl.semaphore_signal(barrier, inc=1, device_id={"seq": to}, device_id_type=MESH)

    for d in range(1, ch_count):
        pl.semaphore_signal(
            barrier, inc=1, device_id={"ch": lax.rem(my_ch + d, ch_count)}, device_id_type=MESH
        )

    for load in loads[0:4]:
        load.wait()
    own = taps_ref[...].astype(f32)
    row_taps[pl.ds(pl.multiple_of(my_y * 8, 8), 8), :] = jnp.concatenate([own, own], axis=0)

    group = LANES // 8
    for c in range(up_ref.shape[1] // LANES):
        cols = pl.ds(c * LANES, LANES)
        product = up_ref[:, cols].astype(f32) * gate_ref[:, cols].astype(f32)
        value = value_ref[:, cols].astype(f32)
        send1[pl.ds(c * group, group)] = jnp.concatenate(
            [product.T.reshape(group, 8, LANES), value.T.reshape(group, 8, LANES)], axis=1
        ).astype(bf16)

    pl.semaphore_wait(barrier, seq_count - 1 + ch_count - 1)

    def send_y(d, carry):
        mine = row_taps.at[pl.ds(pl.multiple_of(my_y * 8, 8), 8)]
        pltpu.make_async_remote_copy(
            src_ref=mine,
            dst_ref=mine,
            send_sem=send_sems.at[0],
            recv_sem=recv_sems.at[0],
            device_id={"seq": my_z * y_count + lax.rem(my_y + d, y_count)},
            device_id_type=MESH,
        ).start()
        return carry

    lax.fori_loop(1, y_count, send_y, 0)

    for to in partners:
        pltpu.make_async_remote_copy(
            src_ref=send1.at[to],
            dst_ref=recv1.at[me],
            send_sem=send_sems.at[1],
            recv_sem=recv_sems.at[1],
            device_id={"seq": to},
            device_id_type=MESH,
        ).start()
    recv1[me] = send1[me]

    def wait_all(ref, sem):
        pltpu.make_async_copy(ref, ref, sem).wait()

    wait_all(row_taps.at[pl.ds(0, (y_count - 1) * 8)], recv_sems.at[0])

    packed_taps[...] = jnp.concatenate(
        [row_taps[pl.ds(f, y_count, stride=8), :] for f in range(filters)], axis=0
    ).astype(bf16)

    def send_z(d, carry):
        pltpu.make_async_remote_copy(
            src_ref=packed_taps,
            dst_ref=all_taps.at[my_z],
            send_sem=send_sems.at[2],
            recv_sem=recv_sems.at[2],
            device_id={"seq": lax.rem(my_z + d, z_count) * y_count + my_y},
            device_id_type=MESH,
        ).start()
        return carry

    lax.fori_loop(1, z_count, send_z, 0)
    all_taps[my_z] = packed_taps[...]

    for load in loads[4:]:
        load.wait()
    slot = lax.broadcasted_iota(jnp.int32, (halves, halves), 0)
    column = lax.broadcasted_iota(jnp.int32, (halves, halves), 1)
    split = (2 * lax.rem(column, blocks) + lax.div(column, blocks) == slot).astype(bf16)
    ids = ids_ref[...].reshape(1, halves).astype(f32).astype(bf16)
    split_ids = jnp.dot(ids, split, preferred_element_type=f32).astype(jnp.int32)
    place = jnp.where(slot == split_ids, 1.0, 0.0)
    chooser, chooser_rows = place.astype(bf16), place.T.astype(bf16)

    def table(start, rows, first=0, columns=tall):
        return matrix[start : start + rows, first : first + columns]

    for n in range(2):
        left[:, n * halves : (n + 1) * halves] = jnp.dot(
            table(0, tall, n * halves, halves), chooser, preferred_element_type=f32
        ).astype(bf16)
        left_back[n] = jnp.dot(
            chooser_rows, table(tall + n * halves, halves), preferred_element_type=f32
        ).astype(bf16)

    taps_tab = table(2 * tall, tall)
    lags_tab = [table(3 * tall + n * halves, halves) for n in range(2)]
    inner_rows, outer_rows = 4 * tall, 4 * tall + 4 * LANES
    inner = [table(inner_rows + n * 2 * LANES, 2 * LANES, 0, 2 * LANES) for n in range(2)]
    outer = [table(outer_rows + n * 2 * LANES, 2 * LANES, 0, 2 * LANES) for n in range(2)]

    low_lane = lax.broadcasted_iota(jnp.int32, (blocks, LANES), 1) < HALF
    top_row = lax.broadcasted_iota(jnp.int32, (halves, LANES), 0) == 0

    def by_halves(rows0, rows1):
        return jnp.concatenate(
            [
                jnp.where(low_lane, rows0, pltpu.roll(rows1, HALF, 1)),
                jnp.where(low_lane, pltpu.roll(rows0, HALF, 1), rows1),
            ],
            axis=0,
        )

    def joined(rows):
        even, odd = rows[0:blocks], rows[blocks : 2 * blocks]
        return (
            jnp.where(low_lane, even, pltpu.roll(odd, HALF, 1)),
            jnp.where(low_lane, pltpu.roll(even, HALF, 1), odd),
        )

    def parts_of(x):
        high = x.astype(bf16)
        return high, (x - high.astype(f32)).astype(bf16)

    def dot(a, b):
        return jnp.dot(a, b, preferred_element_type=f32)

    def product_right(x, table):
        high, rest = parts_of(x)
        return dot(high, table[0]) + dot(high, table[1]) + dot(rest, table[0])

    def product_left(table, x):
        high, rest = parts_of(x)
        return dot(table[0], high) + dot(table[1], high) + dot(table[0], rest)

    def spectrum(re, im):
        cosine, sine = twiddle[0], twiddle[1]
        turned = jnp.concatenate([re * cosine - im * sine, re * sine + im * cosine], axis=1)
        return product_right(turned, inner)

    def conj_times(a, b):
        ar, ai = a[:, 0:LANES], a[:, LANES:]
        br, bi = b[:, 0:LANES], b[:, LANES:]
        return jnp.concatenate([ar * br + ai * bi, ar * bi - ai * br], axis=1)

    def unturned(x):
        y = product_right(x, outer)
        re, im = y[:, 0:LANES], y[:, LANES:]
        cosine, sine = twiddle[0], twiddle[1]
        re, im = re * cosine + im * sine, im * cosine - re * sine
        re, re_pair, im, im_pair = re[0:halves], re[halves:], im[0:halves], im[halves:]
        real = [jnp.where(top_row, re, re + re_pair), jnp.where(top_row, re_pair, im - im_pair)]
        imag = [jnp.where(top_row, im, im + im_pair), jnp.where(top_row, im_pair, re_pair - re)]
        return jnp.concatenate(real, axis=0), jnp.concatenate(imag, axis=0)

    def unfolded(of_real, of_imag=None):
        cos_re, sin_re = of_real[0:halves], of_real[halves:]
        sin_low = jnp.where(top_row, 0.0, sin_re)
        if of_imag is None:
            re = [cos_re, jnp.where(top_row, sin_re, cos_re)]
            im = [sin_low, -sin_low]
        else:
            cos_im, sin_im = of_imag[0:halves], of_imag[halves:]
            re = [
                cos_re - jnp.where(top_row, 0.0, sin_im),
                jnp.where(top_row, sin_re, cos_re + sin_im),
            ]
            im = [cos_im + sin_low, jnp.where(top_row, sin_im, cos_im - sin_re)]
        return jnp.concatenate(re, axis=0), jnp.concatenate(im, axis=0)

    wait_all(recv1.at[pl.ds(0, seq_count - 1)], recv_sems.at[1])
    wide1[...] = recv1[...].astype(f32).reshape(blocks * 16, LANES)

    def first_stage(base):
        data = jnp.concatenate(
            [
                by_halves(
                    wide1[pl.ds(base + a * filters + f, blocks, stride=16), :],
                    wide1[pl.ds(base + a * filters + f + 1, blocks, stride=16), :],
                )
                for a in range(2)
                for f in range(0, filters, 2)
            ],
            axis=1,
        ).astype(bf16)
        return dot(left[...], jnp.concatenate([data, data], axis=0))

    grad_first = first_stage(0)
    value_first = first_stage(8)
    pairs_of_filters = filters // 2
    grad_spectra, lag_back = [], []
    for q in range(pairs_of_filters):
        real = slice(q * LANES, (q + 1) * LANES)
        imag = slice((pairs_of_filters + q) * LANES, (pairs_of_filters + q + 1) * LANES)
        grad_spec = spectrum(*unfolded(grad_first[:, real], grad_first[:, imag]))
        value_spec = spectrum(*unfolded(value_first[:, real], value_first[:, imag]))
        grad_spectra.append(grad_spec)
        lag_back.append(unturned(conj_times(value_spec, grad_spec))[0])
    lag_sums = product_left(lags_tab, jnp.concatenate(lag_back, axis=1)) * scale

    for q in range(filters // 2):
        for n, rows in enumerate(joined(lag_sums[:, q * LANES : (q + 1) * LANES])):
            lag_send[:, 2 * q + n, :] = rows
    for to in partners:
        pltpu.make_async_remote_copy(
            src_ref=lag_send.at[to],
            dst_ref=lag_recv.at[me],
            send_sem=send_sems.at[5],
            recv_sem=recv_sems.at[5],
            device_id={"seq": to},
            device_id_type=MESH,
        ).start()
    lag_recv[me] = lag_send[me]

    wait_all(all_taps.at[pl.ds(0, z_count - 1)], recv_sems.at[2])
    taps_wide = all_taps[...].astype(f32)

    def taps_of(f):
        return taps_wide[:, f * y_count : (f + 1) * y_count, :].reshape(blocks, LANES)

    taps_in = jnp.concatenate(
        [by_halves(taps_of(f), taps_of(f + 1)) for f in range(0, filters, 2)], axis=1
    ).astype(bf16)
    taps_first = dot(taps_tab, jnp.concatenate([taps_in, taps_in], axis=0))
    grad_back = []
    for q in range(filters // 2):
        lanes = slice(q * LANES, (q + 1) * LANES)
        taps_spec = spectrum(*unfolded(taps_first[:, lanes]))
        grad_back.append(unturned(conj_times(taps_spec, grad_spectra[q])))

    folded = [grad_back[q][a] for a in range(2) for q in range(pairs_of_filters)]
    in_grad = product_left(left_back, jnp.concatenate(folded, axis=1)) * scale
    for a in range(2):
        for q in range(pairs_of_filters):
            start = (a * pairs_of_filters + q) * LANES
            for n, rows in enumerate(joined(in_grad[:, start : start + LANES])):
                send2[:, a * filters + 2 * q + n, :] = rows
    for to in partners[::-1]:
        pltpu.make_async_remote_copy(
            src_ref=send2.at[to],
            dst_ref=recv2.at[me],
            send_sem=send_sems.at[3],
            recv_sem=recv_sems.at[3],
            device_id={"seq": to},
            device_id_type=MESH,
        ).start()
    recv2[me] = send2[me]

    wait_all(lag_recv.at[pl.ds(0, seq_count - 1)], recv_sems.at[5])
    part[...] = jnp.sum(lag_recv[...], axis=0)
    for d in range(1, ch_count):
        pltpu.make_async_remote_copy(
            src_ref=part,
            dst_ref=parts.at[my_ch],
            send_sem=send_sems.at[4],
            recv_sem=recv_sems.at[4],
            device_id={"ch": lax.rem(my_ch + d, ch_count)},
            device_id_type=MESH,
        ).start()
    parts[my_ch] = part[...]

    wait_all(recv2.at[pl.ds(0, seq_count - 1)], recv_sems.at[3])
    for c in range(vg_ref.shape[1] // LANES):
        rows = recv2[pl.ds(c * group, group)].reshape(LANES, LANES)
        vg_ref[:, pl.ds(c * LANES, LANES)] = rows.T.astype(bf16)

    wait_all(parts.at[pl.ds(0, ch_count - 1)], recv_sems.at[4])
    fg_ref[...] = jnp.sum(parts[...], axis=0)

    wait_all(row_taps.at[pl.ds(0, (y_count - 1) * 8)], send_sems.at[0])
    wait_all(send1.at[pl.ds(0, seq_count - 1)], send_sems.at[1])
    wait_all(all_taps.at[pl.ds(0, z_count - 1)], send_sems.at[2])
    wait_all(lag_send.at[pl.ds(0, seq_count - 1)], send_sems.at[5])
    wait_all(send2.at[pl.ds(0, seq_count - 1)], send_sems.at[3])
    wait_all(parts.at[pl.ds(0, ch_count - 1)], send_sems.at[4])


def write_out(vg_ref, fg_ref, vg_out, fg_out):
    vg_out[...] = vg_ref[...]
    fg_out[...] = fg_ref[...]


def local(upstream_grad, gate_act, value_act, filter_taps, half_ids):
    seq_count = lax.axis_size("seq")
    ch_count = lax.axis_size("ch")
    local_rows, channels = upstream_grad.shape
    filters = filter_taps.shape[0]
    blocks = seq_count
    halves = 2 * blocks
    tall = 2 * halves
    y_count = 1 << ((seq_count.bit_length() - 1) // 2)
    f32, bf16 = jnp.float32, jnp.bfloat16
    twiddle, pieces = tables(halves)
    width = max(tall, 2 * LANES)
    matrix = np.concatenate([np.pad(x, ((0, 0), (0, width - x.shape[1]))) for x in pieces], 0)
    constants = [jnp.asarray(twiddle), jnp.asarray(matrix)]
    vmem = pl.BlockSpec(memory_space=pltpu.VMEM)
    operands = [upstream_grad, gate_act, value_act, filter_taps, half_ids] + constants
    results = pl.pallas_call(
        functools.partial(kernel, seq_count, ch_count),
        out_shape=(
            pltpu.VMEM((local_rows, channels), bf16),
            pltpu.VMEM((filters, LANES), f32),
        ),
        in_specs=[pl.BlockSpec(memory_space=pl.ANY)] * len(operands),
        out_specs=(vmem, vmem),
        scratch_shapes=[pltpu.VMEM(x.shape, x.dtype) for x in operands]
        + [
            pltpu.VMEM((y_count * 8, LANES), f32),
            pltpu.VMEM((filters * y_count, LANES), bf16),
            pltpu.VMEM((seq_count // y_count, filters * y_count, LANES), bf16),
            pltpu.VMEM((seq_count, 16, LANES), bf16),
            pltpu.VMEM((seq_count, 16, LANES), bf16),
            pltpu.VMEM((blocks * 16, LANES), f32),
            pltpu.VMEM((tall, tall), bf16),
            pltpu.VMEM((2, halves, tall), bf16),
            pltpu.VMEM((seq_count, filters, LANES), f32),
            pltpu.VMEM((seq_count, filters, LANES), f32),
            pltpu.VMEM((seq_count, 8, LANES), f32),
            pltpu.VMEM((seq_count, 8, LANES), f32),
            pltpu.VMEM((filters, LANES), f32),
            pltpu.VMEM((ch_count, filters, LANES), f32),
            pltpu.SemaphoreType.DMA((len(operands),)),
            pltpu.SemaphoreType.DMA((6,)),
            pltpu.SemaphoreType.DMA((6,)),
        ],
        compiler_params=pltpu.CompilerParams(
            collective_id=0, has_side_effects=True, vmem_limit_bytes=60 * 1024 * 1024
        ),
        cost_estimate=pl.CostEstimate(
            flops=40 * 2 * 256**3,
            bytes_accessed=4 * local_rows * channels * 2,
            transcendentals=0,
        ),
    )(*operands)
    return pl.pallas_call(
        write_out,
        out_shape=(
            jax.ShapeDtypeStruct((local_rows, channels), bf16),
            jax.ShapeDtypeStruct((filters, LANES), f32),
        ),
        in_specs=[vmem, vmem],
        out_specs=(vmem, vmem),
        compiler_params=pltpu.CompilerParams(vmem_limit_bytes=1024 * 1024),
    )(*results)


def solution(mesh):
    placed = (P("seq", "ch"), P("seq", "ch"), P("seq", "ch"), P(None, "seq"), P())
    return jax.shard_map(
        local,
        mesh=mesh,
        in_specs=placed,
        out_specs=(P("seq", "ch"), P(None, "seq")),
        check_vma=False,
    )
```

```python
import functools
import math

import jax
import jax.numpy as jnp
import ml_dtypes
import numpy as np
from jax import lax
from jax.experimental import pallas as pl
from jax.experimental.pallas import tpu as pltpu
from jax.sharding import PartitionSpec as P

MESH = pl.DeviceIdType.MESH
LANES = 128
HALF = 64


def two_parts(table):
    high = table.astype(ml_dtypes.bfloat16)
    rest = (table - high.astype(np.float64)).astype(ml_dtypes.bfloat16)
    return high, rest


@functools.lru_cache(maxsize=None)
def tables(halves):
    tall = 2 * halves
    points = tall * HALF
    angle = 2 * np.pi * np.outer(np.arange(halves), np.arange(halves)) / tall
    cosine, sine = np.cos(angle), -np.sin(angle)
    sine[0] = np.cos(np.pi * np.arange(halves))
    both = np.concatenate([cosine, sine], 0)
    natural = np.concatenate([np.arange(0, halves, 2), np.arange(1, halves, 2)])
    forward = np.concatenate(two_parts(both), 1)
    back = np.concatenate(two_parts(both.T), 0)
    taps = np.concatenate(two_parts(both[:, natural]), 1)
    lags = np.concatenate(two_parts(both.T[natural]), 0)
    order = np.concatenate([np.arange(halves + 1), np.arange(tall - 1, halves, -1)])
    turn = 2 * np.pi * np.outer(order, np.arange(HALF)) / points
    turn = np.tile(turn, (1, 2))
    twiddle = np.stack([np.cos(turn), -np.sin(turn)]).astype(np.float32)
    small = 2 * np.pi * np.outer(np.arange(HALF), np.arange(HALF)) / HALF
    pair = np.eye(2)
    real, imag = np.kron(pair, np.cos(small)), np.kron(pair, -np.sin(small))
    inner = two_parts(np.block([[real, imag], [-imag, real]]))
    outer = two_parts(np.block([[real, -imag], [imag, real]]))
    return twiddle, (forward, back, taps, lags) + inner + outer


def kernel(
    seq_count,
    ch_count,
    up_hbm,
    gate_hbm,
    value_hbm,
    taps_hbm,
    ids_hbm,
    twiddle_hbm,
    matrix_hbm,
    vg_ref,
    fg_ref,
    up_ref,
    gate_ref,
    value_ref,
    taps_ref,
    ids_ref,
    twiddle,
    matrix,
    row_taps,
    packed_taps,
    all_taps,
    send1,
    recv1,
    wide1,
    left,
    left_back,
    lag_send,
    lag_recv,
    send2,
    recv2,
    part,
    parts,
    load_sems,
    send_sems,
    recv_sems,
):
    f32, bf16 = jnp.float32, jnp.bfloat16
    y_count = 1 << ((seq_count.bit_length() - 1) // 2)
    z_count = seq_count // y_count
    me = lax.axis_index("seq")
    my_ch = lax.axis_index("ch")
    my_z, my_y = lax.div(me, y_count), lax.rem(me, y_count)
    blocks = seq_count
    halves = 2 * blocks
    tall = 2 * halves
    filters = taps_ref.shape[0]
    scale = 1.0 / math.sqrt(blocks * LANES) / (tall * HALF)

    pairs = (
        (up_hbm, up_ref),
        (gate_hbm, gate_ref),
        (value_hbm, value_ref),
        (taps_hbm, taps_ref),
        (ids_hbm, ids_ref),
        (twiddle_hbm, twiddle),
        (matrix_hbm, matrix),
    )
    loads = [
        pltpu.make_async_copy(src, dst, load_sems.at[i]) for i, (src, dst) in enumerate(pairs)
    ]
    for load in loads:
        load.start()

    steps = sorted(
        ((dz, dy) for dz in range(z_count) for dy in range(y_count) if dz + dy > 0),
        key=lambda step: -min(step[0], z_count - step[0]) - min(step[1], y_count - step[1]),
    )
    partners = [
        lax.rem(my_z + dz, z_count) * y_count + lax.rem(my_y + dy, y_count) for dz, dy in steps
    ]

    barrier = pltpu.get_barrier_semaphore()

    for to in partners:
        pl.semaphore_signal(barrier, inc=1, device_id={"seq": to}, device_id_type=MESH)

    for d in range(1, ch_count):
        pl.semaphore_signal(
            barrier, inc=1, device_id={"ch": lax.rem(my_ch + d, ch_count)}, device_id_type=MESH
        )

    for load in loads[0:4]:
        load.wait()
    own = taps_ref[...].astype(f32)
    row_taps[pl.ds(pl.multiple_of(my_y * 8, 8), 8), :] = jnp.concatenate([own, own], axis=0)

    group = LANES // 8
    for c in range(up_ref.shape[1] // LANES):
        cols = pl.ds(c * LANES, LANES)
        product = up_ref[:, cols].astype(f32) * gate_ref[:, cols].astype(f32)
        value = value_ref[:, cols].astype(f32)
        send1[pl.ds(c * group, group)] = jnp.concatenate(
            [product.T.reshape(group, 8, LANES), value.T.reshape(group, 8, LANES)], axis=1
        ).astype(bf16)

    pl.semaphore_wait(barrier, seq_count - 1 + ch_count - 1)

    def send_y(d, carry):
        mine = row_taps.at[pl.ds(pl.multiple_of(my_y * 8, 8), 8)]
        pltpu.make_async_remote_copy(
            src_ref=mine,
            dst_ref=mine,
            send_sem=send_sems.at[0],
            recv_sem=recv_sems.at[0],
            device_id={"seq": my_z * y_count + lax.rem(my_y + d, y_count)},
            device_id_type=MESH,
        ).start()
        return carry

    lax.fori_loop(1, y_count, send_y, 0)

    for to in partners:
        pltpu.make_async_remote_copy(
            src_ref=send1.at[to],
            dst_ref=recv1.at[me],
            send_sem=send_sems.at[1],
            recv_sem=recv_sems.at[1],
            device_id={"seq": to},
            device_id_type=MESH,
        ).start()
    recv1[me] = send1[me]

    def wait_all(ref, sem):
        pltpu.make_async_copy(ref, ref, sem).wait()

    wait_all(row_taps.at[pl.ds(0, (y_count - 1) * 8)], recv_sems.at[0])

    packed_taps[...] = jnp.concatenate(
        [row_taps[pl.ds(f, y_count, stride=8), :] for f in range(filters)], axis=0
    ).astype(bf16)

    def send_z(d, carry):
        pltpu.make_async_remote_copy(
            src_ref=packed_taps,
            dst_ref=all_taps.at[my_z],
            send_sem=send_sems.at[2],
            recv_sem=recv_sems.at[2],
            device_id={"seq": lax.rem(my_z + d, z_count) * y_count + my_y},
            device_id_type=MESH,
        ).start()
        return carry

    lax.fori_loop(1, z_count, send_z, 0)
    all_taps[my_z] = packed_taps[...]

    for load in loads[4:]:
        load.wait()
    slot = lax.broadcasted_iota(jnp.int32, (halves, halves), 0)
    column = lax.broadcasted_iota(jnp.int32, (halves, halves), 1)
    split = (2 * lax.rem(column, blocks) + lax.div(column, blocks) == slot).astype(bf16)
    ids = ids_ref[...].reshape(1, halves).astype(f32).astype(bf16)
    split_ids = jnp.dot(ids, split, preferred_element_type=f32).astype(jnp.int32)
    place = jnp.where(slot == split_ids, 1.0, 0.0)
    chooser, chooser_rows = place.astype(bf16), place.T.astype(bf16)

    def table(start, rows, first=0, columns=tall):
        return matrix[start : start + rows, first : first + columns]

    for n in range(2):
        left[:, n * halves : (n + 1) * halves] = jnp.dot(
            table(0, tall, n * halves, halves), chooser, preferred_element_type=f32
        ).astype(bf16)
        left_back[n] = jnp.dot(
            chooser_rows, table(tall + n * halves, halves), preferred_element_type=f32
        ).astype(bf16)

    taps_tab = table(2 * tall, tall)
    lags_tab = [table(3 * tall + n * halves, halves) for n in range(2)]
    inner_rows, outer_rows = 4 * tall, 4 * tall + 4 * LANES
    inner = [table(inner_rows + n * 2 * LANES, 2 * LANES, 0, 2 * LANES) for n in range(2)]
    outer = [table(outer_rows + n * 2 * LANES, 2 * LANES, 0, 2 * LANES) for n in range(2)]

    low_lane = lax.broadcasted_iota(jnp.int32, (blocks, LANES), 1) < HALF
    top_row = lax.broadcasted_iota(jnp.int32, (halves, LANES), 0) == 0

    def by_halves(rows0, rows1):
        return jnp.concatenate(
            [
                jnp.where(low_lane, rows0, pltpu.roll(rows1, HALF, 1)),
                jnp.where(low_lane, pltpu.roll(rows0, HALF, 1), rows1),
            ],
            axis=0,
        )

    def joined(rows):
        even, odd = rows[0:blocks], rows[blocks : 2 * blocks]
        return (
            jnp.where(low_lane, even, pltpu.roll(odd, HALF, 1)),
            jnp.where(low_lane, pltpu.roll(even, HALF, 1), odd),
        )

    def parts_of(x):
        high = x.astype(bf16)
        return high, (x - high.astype(f32)).astype(bf16)

    def dot(a, b):
        return jnp.dot(a, b, preferred_element_type=f32)

    def product_right(x, table):
        high, rest = parts_of(x)
        return dot(high, table[0]) + dot(high, table[1]) + dot(rest, table[0])

    def product_left(table, x):
        high, rest = parts_of(x)
        return dot(table[0], high) + dot(table[1], high) + dot(table[0], rest)

    def spectrum(re, im):
        cosine, sine = twiddle[0], twiddle[1]
        turned = jnp.concatenate([re * cosine - im * sine, re * sine + im * cosine], axis=1)
        return product_right(turned, inner)

    def conj_times(a, b):
        ar, ai = a[:, 0:LANES], a[:, LANES:]
        br, bi = b[:, 0:LANES], b[:, LANES:]
        return jnp.concatenate([ar * br + ai * bi, ar * bi - ai * br], axis=1)

    def unturned(x):
        y = product_right(x, outer)
        re, im = y[:, 0:LANES], y[:, LANES:]
        cosine, sine = twiddle[0], twiddle[1]
        re, im = re * cosine + im * sine, im * cosine - re * sine
        re, re_pair, im, im_pair = re[0:halves], re[halves:], im[0:halves], im[halves:]
        real = [jnp.where(top_row, re, re + re_pair), jnp.where(top_row, re_pair, im - im_pair)]
        imag = [jnp.where(top_row, im, im + im_pair), jnp.where(top_row, im_pair, re_pair - re)]
        return jnp.concatenate(real, axis=0), jnp.concatenate(imag, axis=0)

    def unfolded(of_real, of_imag=None):
        cos_re, sin_re = of_real[0:halves], of_real[halves:]
        sin_low = jnp.where(top_row, 0.0, sin_re)
        if of_imag is None:
            re = [cos_re, jnp.where(top_row, sin_re, cos_re)]
            im = [sin_low, -sin_low]
        else:
            cos_im, sin_im = of_imag[0:halves], of_imag[halves:]
            re = [
                cos_re - jnp.where(top_row, 0.0, sin_im),
                jnp.where(top_row, sin_re, cos_re + sin_im),
            ]
            im = [cos_im + sin_low, jnp.where(top_row, sin_im, cos_im - sin_re)]
        return jnp.concatenate(re, axis=0), jnp.concatenate(im, axis=0)

    wait_all(recv1.at[pl.ds(0, seq_count - 1)], recv_sems.at[1])
    wide1[...] = recv1[...].astype(f32).reshape(blocks * 16, LANES)

    def first_stage(base):
        data = jnp.concatenate(
            [
                by_halves(
                    wide1[pl.ds(base + a * filters + f, blocks, stride=16), :],
                    wide1[pl.ds(base + a * filters + f + 1, blocks, stride=16), :],
                )
                for a in range(2)
                for f in range(0, filters, 2)
            ],
            axis=1,
        ).astype(bf16)
        return dot(left[...], jnp.concatenate([data, data], axis=0))

    grad_first = first_stage(0)
    value_first = first_stage(8)
    pairs_of_filters = filters // 2
    grad_spectra, lag_back = [], []
    for q in range(pairs_of_filters):
        real = slice(q * LANES, (q + 1) * LANES)
        imag = slice((pairs_of_filters + q) * LANES, (pairs_of_filters + q + 1) * LANES)
        grad_spec = spectrum(*unfolded(grad_first[:, real], grad_first[:, imag]))
        value_spec = spectrum(*unfolded(value_first[:, real], value_first[:, imag]))
        grad_spectra.append(grad_spec)
        lag_back.append(unturned(conj_times(value_spec, grad_spec))[0])
    lag_sums = product_left(lags_tab, jnp.concatenate(lag_back, axis=1)) * scale

    for q in range(filters // 2):
        for n, rows in enumerate(joined(lag_sums[:, q * LANES : (q + 1) * LANES])):
            lag_send[:, 2 * q + n, :] = rows
    for to in partners:
        pltpu.make_async_remote_copy(
            src_ref=lag_send.at[to],
            dst_ref=lag_recv.at[me],
            send_sem=send_sems.at[5],
            recv_sem=recv_sems.at[5],
            device_id={"seq": to},
            device_id_type=MESH,
        ).start()
    lag_recv[me] = lag_send[me]

    wait_all(all_taps.at[pl.ds(0, z_count - 1)], recv_sems.at[2])
    taps_wide = all_taps[...].astype(f32)

    def taps_of(f):
        return taps_wide[:, f * y_count : (f + 1) * y_count, :].reshape(blocks, LANES)

    taps_in = jnp.concatenate(
        [by_halves(taps_of(f), taps_of(f + 1)) for f in range(0, filters, 2)], axis=1
    ).astype(bf16)
    taps_first = dot(taps_tab, jnp.concatenate([taps_in, taps_in], axis=0))
    grad_back = []
    for q in range(filters // 2):
        lanes = slice(q * LANES, (q + 1) * LANES)
        taps_spec = spectrum(*unfolded(taps_first[:, lanes]))
        grad_back.append(unturned(conj_times(taps_spec, grad_spectra[q])))

    folded = [grad_back[q][a] for a in range(2) for q in range(pairs_of_filters)]
    in_grad = product_left(left_back, jnp.concatenate(folded, axis=1)) * scale
    for a in range(2):
        for q in range(pairs_of_filters):
            start = (a * pairs_of_filters + q) * LANES
            for n, rows in enumerate(joined(in_grad[:, start : start + LANES])):
                send2[:, a * filters + 2 * q + n, :] = rows
    for to in partners:
        pltpu.make_async_remote_copy(
            src_ref=send2.at[to],
            dst_ref=recv2.at[me],
            send_sem=send_sems.at[3],
            recv_sem=recv_sems.at[3],
            device_id={"seq": to},
            device_id_type=MESH,
        ).start()
    recv2[me] = send2[me]

    wait_all(lag_recv.at[pl.ds(0, seq_count - 1)], recv_sems.at[5])
    sums = jnp.sum(lag_recv[...].reshape(seq_count // 2, 2 * filters, LANES), axis=0)
    part[...] = sums[0:filters] + sums[filters:]
    for d in range(1, ch_count):
        pltpu.make_async_remote_copy(
            src_ref=part,
            dst_ref=parts.at[my_ch],
            send_sem=send_sems.at[4],
            recv_sem=recv_sems.at[4],
            device_id={"ch": lax.rem(my_ch + d, ch_count)},
            device_id_type=MESH,
        ).start()
    parts[my_ch] = part[...]

    wait_all(recv2.at[pl.ds(0, seq_count - 1)], recv_sems.at[3])
    for c in range(vg_ref.shape[1] // LANES):
        rows = recv2[pl.ds(c * group, group)].reshape(LANES, LANES)
        vg_ref[:, pl.ds(c * LANES, LANES)] = rows.T.astype(bf16)

    wait_all(parts.at[pl.ds(0, ch_count - 1)], recv_sems.at[4])
    fg_ref[...] = jnp.sum(parts[...], axis=0)

    wait_all(row_taps.at[pl.ds(0, (y_count - 1) * 8)], send_sems.at[0])
    wait_all(send1.at[pl.ds(0, seq_count - 1)], send_sems.at[1])
    wait_all(all_taps.at[pl.ds(0, z_count - 1)], send_sems.at[2])
    wait_all(lag_send.at[pl.ds(0, seq_count - 1)], send_sems.at[5])
    wait_all(send2.at[pl.ds(0, seq_count - 1)], send_sems.at[3])
    wait_all(parts.at[pl.ds(0, ch_count - 1)], send_sems.at[4])


def write_out(vg_ref, fg_ref, vg_out, fg_out):
    vg_out[...] = vg_ref[...]
    fg_out[...] = fg_ref[...]


def local(upstream_grad, gate_act, value_act, filter_taps, half_ids):
    seq_count = lax.axis_size("seq")
    ch_count = lax.axis_size("ch")
    local_rows, channels = upstream_grad.shape
    filters = filter_taps.shape[0]
    blocks = seq_count
    halves = 2 * blocks
    tall = 2 * halves
    y_count = 1 << ((seq_count.bit_length() - 1) // 2)
    f32, bf16 = jnp.float32, jnp.bfloat16
    twiddle, pieces = tables(halves)
    width = max(tall, 2 * LANES)
    matrix = np.concatenate([np.pad(x, ((0, 0), (0, width - x.shape[1]))) for x in pieces], 0)
    constants = [jnp.asarray(twiddle), jnp.asarray(matrix)]
    vmem = pl.BlockSpec(memory_space=pltpu.VMEM)
    operands = [upstream_grad, gate_act, value_act, filter_taps, half_ids] + constants
    results = pl.pallas_call(
        functools.partial(kernel, seq_count, ch_count),
        out_shape=(
            pltpu.VMEM((local_rows, channels), bf16),
            pltpu.VMEM((filters, LANES), f32),
        ),
        in_specs=[pl.BlockSpec(memory_space=pl.ANY)] * len(operands),
        out_specs=(vmem, vmem),
        scratch_shapes=[pltpu.VMEM(x.shape, x.dtype) for x in operands]
        + [
            pltpu.VMEM((y_count * 8, LANES), f32),
            pltpu.VMEM((filters * y_count, LANES), bf16),
            pltpu.VMEM((seq_count // y_count, filters * y_count, LANES), bf16),
            pltpu.VMEM((seq_count, 16, LANES), bf16),
            pltpu.VMEM((seq_count, 16, LANES), bf16),
            pltpu.VMEM((blocks * 16, LANES), f32),
            pltpu.VMEM((tall, tall), bf16),
            pltpu.VMEM((2, halves, tall), bf16),
            pltpu.VMEM((seq_count, filters, LANES), f32),
            pltpu.VMEM((seq_count, filters, LANES), f32),
            pltpu.VMEM((seq_count, 8, LANES), f32),
            pltpu.VMEM((seq_count, 8, LANES), f32),
            pltpu.VMEM((filters, LANES), f32),
            pltpu.VMEM((ch_count, filters, LANES), f32),
            pltpu.SemaphoreType.DMA((len(operands),)),
            pltpu.SemaphoreType.DMA((6,)),
            pltpu.SemaphoreType.DMA((6,)),
        ],
        compiler_params=pltpu.CompilerParams(
            collective_id=0, has_side_effects=True, vmem_limit_bytes=60 * 1024 * 1024
        ),
        cost_estimate=pl.CostEstimate(
            flops=40 * 2 * 256**3,
            bytes_accessed=4 * local_rows * channels * 2,
            transcendentals=0,
        ),
    )(*operands)
    return pl.pallas_call(
        write_out,
        out_shape=(
            jax.ShapeDtypeStruct((local_rows, channels), bf16),
            jax.ShapeDtypeStruct((filters, LANES), f32),
        ),
        in_specs=[vmem, vmem],
        out_specs=(vmem, vmem),
        compiler_params=pltpu.CompilerParams(vmem_limit_bytes=1024 * 1024),
    )(*results)


def solution(mesh):
    placed = (P("seq", "ch"), P("seq", "ch"), P("seq", "ch"), P(None, "seq"), P())
    return jax.shard_map(
        local,
        mesh=mesh,
        in_specs=placed,
        out_specs=(P("seq", "ch"), P(None, "seq")),
        check_vma=False,
    )
```
